32 devices in a mesh: grp: 2 (over x), img: 16 (over z, y, core).
Axes of the slice: x: 2, y: 2, z: 4, core: 2. Of those that a mesh axis runs over, the one named last changes fastest.
Arguments:
- particles: bfloat16 [64, 256, 512], P(('grp', 'img')), parts along dimension 0, may hold values from -6 to 6
- whitening: float32 [256], replicated, may hold values from 0.5 to 2
- ctf: float32 [16, 256], P('grp'), parts along dimension 0, may hold values from -1 to 1
- group_id: int32 [64], P(('grp', 'img')), parts along dimension 0, may hold values from 0 to 7
- noise_var: float32 [16], P('grp'), parts along dimension 0, may hold values from 0.1 to 1
- bessel: bfloat16 [128, 64, 256], replicated, may hold values from -0.375 to 0.375
Outputs:
- cleaned: bfloat16 [64, 256, 512], P(('grp', 'img')), parts along dimension 0
The draws below stay inside these ranges and needn't reach their ends.
There are 2 independent parts, one for each index of `grp`. The reference program is written for one: setup_inputs(seed, part) draws one part's arguments, and reference() takes and returns one part's arrays. A program takes and returns all parts, laid end to end along the dimension named above; an argument that names none is the same for every part. Nothing has to cross between parts.
All inputs are finite; a program needn't handle non-finite values.
Results may differ from the reference program's by a relative error of at most 0.0087.
Values may be sent and summed in bfloat16 or wider, within the bound.
A program may use at most 64 MiB of HBM per device.

```python
import math
import jax
import jax.numpy as jnp
from jax import lax

NR = 256
NA = 512
K = 128
Q = 64
GROUPS = 8
NIMG = 32


def place_ends(values, own_key, smallest, top_value):
    shape = values.shape
    spot = [jax.random.randint(jax.random.fold_in(own_key, axis), (), 0, shape[axis]) for axis in range(len(shape))]
    values = values.at[tuple(spot)].set(smallest)
    longest = shape.index(max(shape))
    spot[longest] = (spot[longest] + 1) % shape[longest]
    return values.at[tuple(spot)].set(top_value)


def levels(key, shape, shards, smallest, top_value):
    def one(dim, parts):
        draws = jax.random.uniform(jax.random.fold_in(jax.random.fold_in(key, 6), dim), (parts,), jnp.float32, smallest / len(shards), top_value / len(shards))
        return jnp.repeat(jnp.exp(draws), shape[dim] // parts).reshape((-1,) + (1,) * (len(shape) - dim - 1))

    factor_of = one(*shards[0])
    for cut in shards[1:]:
        factor_of = factor_of * one(*cut)
    return factor_of


def centred(stream_key, shape, width, reach, cuts=(), held_as=jnp.bfloat16):
    entries = jax.random.normal(stream_key, shape, jnp.float32) * width
    if len(cuts) > 0:
        entries = levels(stream_key, shape, cuts, -0.22, 0.18) * entries
    return jnp.clip(entries, min=-reach, max=reach).astype(held_as)


def setup_inputs(seed: int = 0, part: int = 0) -> dict:
    keys = jax.random.split(jax.random.key(seed), 7)
    part_keys = jax.random.split(jax.random.fold_in(keys[6], part), 7)
    particles = centred(part_keys[0], (NIMG, NR, NA), 1.0, 6.0, ((0, 16),))
    whitening = jnp.clip(jnp.exp(jax.random.uniform(keys[1], (NR,), jnp.float32, math.log(0.5), math.log(2.0))), 0.5, 2.0)
    ctf = jnp.clip(jax.random.uniform(part_keys[2], (GROUPS, NR), jnp.float32, -1.0, 1.0), -1.0, 1.0)
    group_id = place_ends(jax.random.randint(part_keys[3], (NIMG,), 0, GROUPS), jax.random.fold_in(part_keys[3], 1), 0, GROUPS - 1).astype(jnp.int32)
    noise_var = jnp.clip(jnp.exp(jax.random.uniform(part_keys[4], (GROUPS,), jnp.float32, math.log(0.1), math.log(1.0))), 0.1, 1.0)
    bessel = centred(keys[5], (K, Q, NR), NR ** -0.5, 0.375)
    return dict(particles=particles, whitening=whitening, ctf=ctf, group_id=group_id, noise_var=noise_var, bessel=bessel)


prior_weight = 8.0

def angle_table(angles, freqs):
    theta = jnp.arange(angles, dtype=jnp.int32)
    order = jnp.arange(freqs, dtype=jnp.int32)
    phase = 2.0 * math.pi / angles * (theta[:, None] * order[None, :] % angles).astype(jnp.float32)
    scale = 1.0 / math.sqrt(angles)
    return jnp.stack([jnp.cos(phase) * scale, -jnp.sin(phase) * scale], axis=1).astype(jnp.bfloat16)

def filter_block(block, labels, counts, noise_var):
    radial = block.shape[-1]
    groups = labels.shape[1]
    rows = block.reshape(-1, radial)
    spread = (rows[:, None, :] * labels[:, :, None]).reshape(rows.shape[0], groups * radial)
    gram = lax.dot_general(spread.astype(jnp.float32), rows.astype(jnp.float32), (((0,), (0,)), ((), ())), preferred_element_type=jnp.float32)
    gram = gram.reshape(groups, radial, radial)
    pooled = lax.optimization_barrier(jnp.sum(gram, axis=0)) / (rows.shape[0] // 2)
    cov = (gram + prior_weight * pooled[None]) / (counts + prior_weight)[:, None, None]
    eye = jnp.eye(radial, dtype=jnp.float32)
    system = cov + noise_var[:, None, None] * eye[None]
    factor = jnp.linalg.cholesky(system)
    lower_inv = lax.linalg.triangular_solve(factor, jnp.broadcast_to(eye, system.shape), left_side=True, lower=True)
    inverse = jnp.einsum('gsq,gst->gqt', lower_inv, lower_inv, precision=lax.Precision.HIGHEST)
    wiener = (eye[None] - noise_var[:, None, None] * inverse).astype(jnp.bfloat16)
    weights = wiener.transpose(2, 0, 1).reshape(radial, groups * radial)
    mixed = jnp.dot(rows.astype(jnp.float32), weights.astype(jnp.float32), preferred_element_type=jnp.float32).reshape(rows.shape[0], groups, radial)
    applied = lax.optimization_barrier(jnp.sum(mixed * labels.astype(jnp.float32)[:, :, None], axis=1)).astype(jnp.bfloat16)
    return applied.reshape(block.shape)

def reference(particles, whitening, ctf, group_id, noise_var, bessel):
    onehot = (group_id[:, None] == jnp.arange(GROUPS, dtype=jnp.int32)[None, :]).astype(jnp.float32)
    weight_rows = jnp.dot(onehot, ctf, precision=lax.Precision.HIGHEST) * whitening[None, :]
    filtered = (particles.astype(jnp.float32) * weight_rows[:, :, None]).astype(jnp.bfloat16)
    table = angle_table(NA, K)
    spectrum = jnp.dot(filtered.reshape(NIMG * NR, NA).astype(jnp.float32), table.reshape(NA, 2 * K).astype(jnp.float32), preferred_element_type=jnp.float32)
    spectrum = spectrum.astype(jnp.bfloat16).reshape(NIMG, NR, 2, K)
    coef = jnp.einsum('irpk,kqr->kipq', spectrum.astype(jnp.float32), bessel.astype(jnp.float32)).astype(jnp.bfloat16)
    counts = lax.optimization_barrier(jnp.sum(onehot, axis=0))
    labels = jnp.repeat(onehot, 2, axis=0).astype(jnp.bfloat16)
    denoised = lax.map(lambda block: filter_block(block, labels, counts, noise_var), coef)
    back = jnp.einsum('kipq,kqr->irpk', denoised.astype(jnp.float32), bessel.astype(jnp.float32)).astype(jnp.bfloat16)
    cleaned = jnp.dot(back.reshape(NIMG * NR, 2 * K).astype(jnp.float32), table.reshape(NA, 2 * K).T.astype(jnp.float32), preferred_element_type=jnp.float32)
    return cleaned.astype(jnp.bfloat16).reshape(NIMG, NR, NA)
```

```python
import functools
import math

import jax
import jax.numpy as jnp
from jax import lax
from jax.experimental import pallas as pl
from jax.experimental.pallas import tpu as pltpu
from jax.sharding import PartitionSpec as P

prior_weight = 8.0
SLOTS = 64
LANES = 2 * SLOTS
TILE = 8


def angle_table(angles, freqs):
    theta = jnp.arange(angles, dtype=jnp.int32)
    order = jnp.arange(freqs, dtype=jnp.int32)
    phase = 2.0 * math.pi / angles * (theta[:, None] * order[None, :] % angles).astype(jnp.float32)
    scale = 1.0 / math.sqrt(angles)
    return jnp.stack([jnp.cos(phase) * scale, -jnp.sin(phase) * scale], axis=1).astype(jnp.bfloat16)


def nt_dot(a, b):
    return lax.dot_general(a, b, (((1,), (1,)), ((), ())), preferred_element_type=jnp.float32)


def swap_halves(x):
    return pltpu.roll(x, SLOTS, x.ndim - 1)


def sweep_all(a_ref, c_ref, v_ref, q):
    hq = q // 2
    half = lax.broadcasted_iota(jnp.int32, (TILE, LANES), 1) // SLOTS
    half_w = lax.broadcasted_iota(jnp.int32, (hq, LANES), 1) // SLOTS
    sub_w = lax.broadcasted_iota(jnp.int32, (hq, LANES), 0)
    for kb in range(q // TILE):
        h, base = divmod(kb * TILE, hq)
        in_half = half == h
        rows = [a_ref[kb * TILE + t] for t in range(TILE)]
        for t in range(TILE):
            row = rows[t]
            turned = swap_halves(row)
            c_ref[t, 0:hq] = jnp.where(half_w == 0, row, turned)
            c_ref[t, hq:q] = jnp.where(half_w == 1, row, turned)
            own = jnp.where(in_half, row[base:base + TILE], turned[base:base + TILE])
            inv = 1.0 / own[t:t + 1]
            here = (half_w == h) & (sub_w == base + t)
            scaled = jnp.where(here, -inv, row * inv)
            later = (half_w == h) & (sub_w > base + t) & (sub_w < base + TILE)
            v_ref[t] = jnp.where(later, 0.0, scaled)
            for u in range(TILE):
                if u != t:
                    rows[u] = jnp.where(here, 0.0, rows[u]) - own[u:u + 1] * scaled
            rows[t] = scaled
        vs = [v_ref[t] for t in range(TILE)]
        keep = ~((half_w == h) & (sub_w >= base) & (sub_w < base + TILE))

        def update(i, carry):
            acc = jnp.where(keep, a_ref[i], 0.0)
            for t in range(TILE):
                acc = acc - c_ref[t, pl.ds(i, 1), :] * vs[t]
            a_ref[i] = acc
            return carry

        lax.fori_loop(0, q, update, 0, unroll=4)
        for t in range(TILE):
            a_ref[kb * TILE + t] = rows[t]


def filter_kernel(groups, imgs, coef_ref, bid_ref, kid_ref, noise_ref, out_ref, cf_ref, a_ref, c_ref, v_ref, d_ref):
    q, width = coef_ref.shape
    hq = q // 2
    slot = lax.broadcasted_iota(jnp.int32, (LANES, width), 0)
    member = (slot % SLOTS == bid_ref[...]).astype(jnp.float32)
    same = (slot % SLOTS // groups == kid_ref[...]).astype(jnp.float32)
    low = slot < SLOTS
    weights = member + same * (prior_weight / imgs)
    w_lo = jnp.where(low, weights, 0.0).astype(jnp.bfloat16)
    w_hi = jnp.where(low, 0.0, weights).astype(jnp.bfloat16)
    counts = nt_dot(jnp.full((TILE, width), 0.5, jnp.bfloat16), member.astype(jnp.bfloat16))[0:1]
    scale = 1.0 / (counts + prior_weight)
    noise = noise_ref[...]
    cf_ref[...] = coef_ref[...].astype(jnp.float32)
    jj = lax.broadcasted_iota(jnp.int32, (hq, LANES), 0)
    col = jj + hq * (lax.broadcasted_iota(jnp.int32, (hq, LANES), 1) // SLOTS)

    def gram(blk, carry):
        start = pl.multiple_of(blk * TILE, TILE)
        mine = cf_ref[pl.ds(start, TILE), :]
        total = None
        for part, w in ((0, w_lo), (1, w_hi)):
            other = cf_ref[part * hq:(part + 1) * hq, :]
            prod = (mine[:, None, :] * other[None, :, :]).reshape(TILE * hq, width)
            top = prod.astype(jnp.bfloat16)
            rest = (prod - top.astype(jnp.float32)).astype(jnp.bfloat16)
            s = nt_dot(top, w) + nt_dot(rest, w)
            total = s if total is None else total + s
        total = total.reshape(TILE, hq, LANES) * scale[None]
        for t in range(TILE):
            a_ref[start + t] = total[t] + jnp.where(col == start + t, noise, 0.0)
        return carry

    lax.fori_loop(0, q // TILE, gram, 0)
    sweep_all(a_ref, c_ref, v_ref, q)
    e_lo = jnp.where(low, member, 0.0).astype(jnp.bfloat16)
    e_hi = jnp.where(low, 0.0, member).astype(jnp.bfloat16)

    def apply(blk, carry):
        start = pl.multiple_of(blk * TILE, TILE)
        wien = []
        for t in range(TILE):
            wien.append(noise * a_ref[start + t] + jnp.where(col == start + t, 1.0, 0.0))
        wien = jnp.concatenate(wien, axis=0).astype(jnp.bfloat16)
        spread_lo = jnp.dot(wien, e_lo, preferred_element_type=jnp.float32).reshape(TILE, hq, width)
        spread_hi = jnp.dot(wien, e_hi, preferred_element_type=jnp.float32).reshape(TILE, hq, width)
        prod = spread_lo * cf_ref[0:hq, :][None] + spread_hi * cf_ref[hq:q, :][None]
        d_ref[pl.ds(start, TILE), :] = jnp.sum(prod, axis=1)
        return carry

    lax.fori_loop(0, q // TILE, apply, 0)
    out_ref[...] = d_ref[...].astype(jnp.bfloat16)


def wiener_filter(coef, bid, kid, noise, groups, imgs):
    q, width = coef.shape
    hq = q // 2
    return pl.pallas_call(
        functools.partial(filter_kernel, groups, imgs),
        out_shape=jax.ShapeDtypeStruct((q, width), jnp.bfloat16),
        in_specs=[pl.BlockSpec(memory_space=pltpu.VMEM)] * 4,
        out_specs=pl.BlockSpec(memory_space=pltpu.VMEM),
        scratch_shapes=[
            pltpu.VMEM((q, width), jnp.float32),
            pltpu.VMEM((q, hq, LANES), jnp.float32),
            pltpu.VMEM((TILE, q, LANES), jnp.float32),
            pltpu.VMEM((TILE, hq, LANES), jnp.float32),
            pltpu.VMEM((q, width), jnp.float32),
        ],
        compiler_params=pltpu.CompilerParams(vmem_limit_bytes=32 * 1024 * 1024),
        name="wiener_filter",
    )(coef, bid, kid, noise)


def body(particles, whitening, ctf, group_id, noise_var, bessel):
    img_count, radii, angles = particles.shape
    freqs, radial = bessel.shape[:2]
    groups = ctf.shape[0]
    shards = lax.axis_size("img")
    per_shard = freqs // shards
    imgs = shards * img_count
    group_range = jnp.arange(groups, dtype=jnp.int32)
    onehot_local = (group_id[:, None] == group_range[None, :]).astype(jnp.float32)
    weight_rows = jnp.dot(onehot_local, ctf, precision=lax.Precision.HIGHEST) * whitening[None, :]
    filtered = (particles.astype(jnp.float32) * weight_rows[:, :, None]).astype(jnp.bfloat16)
    table = angle_table(angles, freqs)
    spectrum = jnp.dot(
        filtered.reshape(img_count * radii, angles),
        table.reshape(angles, 2 * freqs),
        preferred_element_type=jnp.float32,
    )
    spectrum = spectrum.astype(jnp.bfloat16).reshape(img_count, radii, 2, freqs)
    all_ids = lax.all_gather(group_id, "img", axis=0, tiled=True)
    first = lax.axis_index("img") * per_shard
    own_tables = lax.dynamic_slice_in_dim(bessel, first, per_shard, 0)
    payload = spectrum.transpose(3, 0, 2, 1)
    arrived = lax.all_to_all(payload, "img", split_axis=0, concat_axis=1, tiled=True)
    coef = jnp.einsum(
        "kqr,kipr->qkip", own_tables, arrived, preferred_element_type=jnp.float32
    ).astype(jnp.bfloat16)
    kid = jnp.repeat(jnp.arange(per_shard, dtype=jnp.int32), 2 * imgs)[None, :]
    bid = kid * groups + jnp.tile(jnp.repeat(all_ids, 2), per_shard)[None, :]
    noise = jnp.tile(noise_var, LANES // groups)[None, :]
    denoised = wiener_filter(
        coef.reshape(radial, per_shard * 2 * imgs), bid, kid, noise, groups, imgs
    ).reshape(radial, per_shard, imgs, 2)
    outgoing = jnp.einsum(
        "qkip,kqr->kipr", denoised, own_tables, preferred_element_type=jnp.float32
    ).astype(jnp.bfloat16)
    returned = lax.all_to_all(outgoing, "img", split_axis=1, concat_axis=0, tiled=True)
    back = returned.transpose(1, 3, 2, 0)
    cleaned = jnp.dot(
        back.reshape(img_count * radii, 2 * freqs),
        table.reshape(angles, 2 * freqs).T,
        preferred_element_type=jnp.float32,
    )
    return cleaned.astype(jnp.bfloat16).reshape(img_count, radii, angles)


def solution(mesh):
    in_specs = (
        P(("grp", "img"), None, None),
        P(),
        P("grp", None),
        P(("grp", "img")),
        P("grp"),
        P(),
    )
    out_specs = P(("grp", "img"), None, None)
    return jax.shard_map(body, mesh=mesh, in_specs=in_specs, out_specs=out_specs, check_vma=False)
```

```python
import functools
import math

import jax
import jax.numpy as jnp
import numpy as np
from jax import lax
from jax.experimental import pallas as pl
from jax.experimental.pallas import tpu as pltpu
from jax.sharding import PartitionSpec as P

prior_weight = 8.0
SLOTS = 64
LANES = 2 * SLOTS
TILE = 8


def angle_table(angles, freqs):
    theta = jnp.arange(angles, dtype=jnp.int32)
    order = jnp.arange(freqs, dtype=jnp.int32)
    phase = 2.0 * math.pi / angles * (theta[:, None] * order[None, :] % angles).astype(jnp.float32)
    scale = 1.0 / math.sqrt(angles)
    return jnp.stack([jnp.cos(phase) * scale, -jnp.sin(phase) * scale], axis=1).astype(jnp.bfloat16)


def nt_dot(a, b):
    return lax.dot_general(a, b, (((1,), (1,)), ((), ())), preferred_element_type=jnp.float32)


def swap_halves(x):
    return pltpu.roll(x, SLOTS, x.ndim - 1)


def sweep_all(a_ref, c_ref, v_ref, q):
    hq = q // 2
    half = lax.broadcasted_iota(jnp.int32, (TILE, LANES), 1) // SLOTS
    half_w = lax.broadcasted_iota(jnp.int32, (hq, LANES), 1) // SLOTS
    sub_w = lax.broadcasted_iota(jnp.int32, (hq, LANES), 0)
    for kb in range(q // TILE):
        h, base = divmod(kb * TILE, hq)
        in_half = half == h
        rows = [a_ref[kb * TILE + t] for t in range(TILE)]
        for t in range(TILE):
            row = rows[t]
            turned = swap_halves(row)
            c_ref[t, 0:hq] = jnp.where(half_w == 0, row, turned)
            c_ref[t, hq:q] = jnp.where(half_w == 1, row, turned)
            own = jnp.where(in_half, row[base:base + TILE], turned[base:base + TILE])
            inv = 1.0 / own[t:t + 1]
            here = (half_w == h) & (sub_w == base + t)
            scaled = jnp.where(here, -inv, row * inv)
            later = (half_w == h) & (sub_w > base + t) & (sub_w < base + TILE)
            v_ref[t] = jnp.where(later, 0.0, scaled)
            for u in range(TILE):
                if u != t:
                    rows[u] = jnp.where(here, 0.0, rows[u]) - own[u:u + 1] * scaled
            rows[t] = scaled
        vs = [v_ref[t] for t in range(TILE)]
        keep = ~((half_w == h) & (sub_w >= base) & (sub_w < base + TILE))

        def update(i, carry):
            acc = jnp.where(keep, a_ref[i], 0.0)
            for t in range(TILE):
                acc = acc - c_ref[t, pl.ds(i, 1), :] * vs[t]
            a_ref[i] = acc
            return carry

        lax.fori_loop(0, q, update, 0, unroll=4)
        for t in range(TILE):
            a_ref[kb * TILE + t] = rows[t]


def filter_kernel(groups, imgs, coef_ref, bid_ref, kid_ref, noise_ref, out_ref, *scratch):
    coef = coef_ref[...].astype(jnp.float32)
    done = filter_lanes(groups, imgs, coef, bid_ref[...], kid_ref[...], noise_ref[...], *scratch)
    out_ref[...] = done.astype(jnp.bfloat16)


def filter_lanes(groups, imgs, coef, bid, kid, noise, cf_ref, a_ref, c_ref, v_ref, d_ref):
    q, width = coef.shape
    hq = q // 2
    slot = lax.broadcasted_iota(jnp.int32, (LANES, width), 0)
    member = (slot % SLOTS == bid).astype(jnp.float32)
    same = (slot % SLOTS // groups == kid).astype(jnp.float32)
    low = slot < SLOTS
    weights = member + same * (prior_weight / imgs)
    w_lo = jnp.where(low, weights, 0.0).astype(jnp.bfloat16)
    w_hi = jnp.where(low, 0.0, weights).astype(jnp.bfloat16)
    counts = nt_dot(jnp.full((TILE, width), 0.5, jnp.bfloat16), member.astype(jnp.bfloat16))[0:1]
    scale = 1.0 / (counts + prior_weight)
    cf_ref[...] = coef
    jj = lax.broadcasted_iota(jnp.int32, (hq, LANES), 0)
    col = jj + hq * (lax.broadcasted_iota(jnp.int32, (hq, LANES), 1) // SLOTS)

    def gram(blk, carry):
        start = pl.multiple_of(blk * TILE, TILE)
        mine = cf_ref[pl.ds(start, TILE), :]
        total = None
        for part, w in ((0, w_lo), (1, w_hi)):
            other = cf_ref[part * hq:(part + 1) * hq, :]
            prod = (mine[:, None, :] * other[None, :, :]).reshape(TILE * hq, width)
            top = prod.astype(jnp.bfloat16)
            rest = (prod - top.astype(jnp.float32)).astype(jnp.bfloat16)
            s = nt_dot(top, w) + nt_dot(rest, w)
            total = s if total is None else total + s
        total = total.reshape(TILE, hq, LANES) * scale[None]
        for t in range(TILE):
            a_ref[start + t] = total[t] + jnp.where(col == start + t, noise, 0.0)
        return carry

    lax.fori_loop(0, q // TILE, gram, 0)
    sweep_all(a_ref, c_ref, v_ref, q)
    e_lo = jnp.where(low, member, 0.0).astype(jnp.bfloat16)
    e_hi = jnp.where(low, 0.0, member).astype(jnp.bfloat16)

    def apply(blk, carry):
        start = pl.multiple_of(blk * TILE, TILE)
        wien = []
        for t in range(TILE):
            wien.append(noise * a_ref[start + t] + jnp.where(col == start + t, 1.0, 0.0))
        wien = jnp.concatenate(wien, axis=0).astype(jnp.bfloat16)
        spread_lo = jnp.dot(wien, e_lo, preferred_element_type=jnp.float32).reshape(TILE, hq, width)
        spread_hi = jnp.dot(wien, e_hi, preferred_element_type=jnp.float32).reshape(TILE, hq, width)
        prod = spread_lo * cf_ref[0:hq, :][None] + spread_hi * cf_ref[hq:q, :][None]
        d_ref[pl.ds(start, TILE), :] = jnp.sum(prod, axis=1)
        return carry

    lax.fori_loop(0, q // TILE, apply, 0)
    return d_ref[...]


def filter_scratch(q, width):
    hq = q // 2
    return [
        pltpu.VMEM((q, width), jnp.float32),
        pltpu.VMEM((q, hq, LANES), jnp.float32),
        pltpu.VMEM((TILE, q, LANES), jnp.float32),
        pltpu.VMEM((TILE, hq, LANES), jnp.float32),
        pltpu.VMEM((q, width), jnp.float32),
    ]


VM = pl.BlockSpec(memory_space=pltpu.VMEM)
PARAMS = pltpu.CompilerParams(vmem_limit_bytes=32 * 1024 * 1024)


def wiener_filter(coef, bid, kid, noise, groups, imgs):
    q, width = coef.shape
    return pl.pallas_call(
        functools.partial(filter_kernel, groups, imgs),
        out_shape=jax.ShapeDtypeStruct((q, width), jnp.bfloat16),
        in_specs=[VM] * 4,
        out_specs=VM,
        scratch_shapes=filter_scratch(q, width),
        compiler_params=PARAMS,
        name="wiener_filter",
    )(coef, bid, kid, noise)


PACK = 4
SHARE = 128 // PACK


def lane_block(shape):
    return lax.broadcasted_iota(jnp.int32, shape, 1) // SHARE


def pack(tile):
    step = tile.shape[0] // PACK
    where = lane_block((step, 128))
    blocks = []
    for peer in range(PACK):
        out = None
        for j in range(PACK):
            piece = tile[j * step:(j + 1) * step]
            turn = (j - peer) * SHARE % 128
            piece = pltpu.roll(piece, turn, 1) if turn else piece
            out = piece if out is None else jnp.where(where == j, piece, out)
        blocks.append(out)
    return blocks


def unpack(blocks):
    step = blocks[0].shape[0]
    where = lane_block((step, 128))
    rows = []
    for j in range(PACK):
        out = None
        for peer in range(PACK):
            turn = (peer - j) * SHARE % 128
            piece = pltpu.roll(blocks[peer], turn, 1) if turn else blocks[peer]
            out = piece if out is None else jnp.where(where == peer, piece, out)
        rows.append(out)
    return jnp.concatenate(rows, axis=0)


def project_kernel(per_shard, gid_ref, part_ref, table_ref, ctf_ref, white_ref, bessel_ref, out_ref, bess, sem):
    images = part_ref.shape[0]
    freqs, q, radii = bess.shape
    shards = freqs // per_shard
    fetch = pltpu.make_async_copy(bessel_ref, bess, sem)
    fetch.start()
    table = table_ref[...]
    half = 2 * per_shard
    spec = []
    for i in range(images):
        weight = ctf_ref[pl.ds(gid_ref[i], 1), :] * white_ref[...]
        spec.append((nt_dot(table, part_ref[i]) * weight).astype(jnp.bfloat16))
    lane = lax.broadcasted_iota(jnp.int32, (q, 128), 1)
    lane_row = lax.broadcasted_iota(jnp.int32, (q // PACK, 128), 1) % SHARE // half
    labels = jnp.zeros((q // PACK, 128), jnp.float32)
    for i in range(images):
        labels = jnp.where(lane_row == i, gid_ref[i].astype(jnp.float32), labels)
    labels = labels.astype(jnp.bfloat16)
    fetch.wait()
    for t in range(shards // PACK):
        rows = []
        for peer in range(PACK):
            d = t * PACK + peer
            for i in range(images):
                rows.append(spec[i][d * half:(d + 1) * half])
        rows = jnp.concatenate(rows, axis=0)
        acc = jnp.zeros((q, 128), jnp.float32)
        for peer in range(PACK):
            d = t * PACK + peer
            block = bess[d * per_shard:(d + 1) * per_shard].reshape(per_shard * q, radii)
            prod = nt_dot(block, rows)
            for kk in range(per_shard):
                here = (lane // SHARE == peer) & (lane % per_shard == kk)
                acc = jnp.where(here, prod[kk * q:(kk + 1) * q], acc)
        for peer, block in enumerate(pack(acc)):
            d = t * PACK + peer
            out_ref[d, 0:q // PACK] = block.astype(jnp.bfloat16)
            out_ref[d, q // PACK:] = labels


def packed_filter_kernel(groups, imgs, per_shard, in_ref, noise_ref, out_ref, *scratch):
    shards, step = in_ref.shape[0], in_ref.shape[1] // 2
    coef, ids = [], []
    for t in range(shards // PACK):
        blocks = [in_ref[t * PACK + peer].astype(jnp.float32) for peer in range(PACK)]
        coef.append(unpack([block[:step] for block in blocks]))
        row = blocks[0][step:step + 1]
        for peer in range(1, PACK):
            row = jnp.where(lane_block((1, 128)) == peer, blocks[peer][step:step + 1], row)
        ids.append(row)
    coef = jnp.concatenate(coef, axis=1)
    ids = jnp.concatenate(ids, axis=1).astype(jnp.int32)
    kid = lax.broadcasted_iota(jnp.int32, ids.shape, 1) % per_shard
    done = filter_lanes(groups, imgs, coef, kid * groups + ids, kid, noise_ref[...], *scratch)
    for t in range(shards // PACK):
        for peer, block in enumerate(pack(done[:, t * 128:(t + 1) * 128])):
            out_ref[t * PACK + peer] = block.astype(jnp.bfloat16)


def restore_kernel(per_shard, in_ref, table_ref, bessel_ref, out_ref, bess, sem):
    shards = in_ref.shape[0]
    images = out_ref.shape[0]
    q, radii = bess.shape[1:]
    fetch = pltpu.make_async_copy(bessel_ref, bess, sem)
    fetch.start()
    half = 2 * per_shard
    span = per_shard * q
    keep = (
        lax.broadcasted_iota(jnp.int32, (SHARE, span), 0) % per_shard
        == lax.broadcasted_iota(jnp.int32, (SHARE, span), 1) // q
    )
    left = []
    for t in range(shards // PACK):
        tile = unpack([in_ref[t * PACK + peer].astype(jnp.float32) for peer in range(PACK)])
        flat = jnp.transpose(tile)
        for peer in range(PACK):
            mine = flat[peer * SHARE:(peer + 1) * SHARE]
            wide = jnp.concatenate([mine] * per_shard, axis=1)
            left.append(jnp.where(keep, wide, 0.0).astype(jnp.bfloat16))
    fetch.wait()
    back = []
    for d in range(shards):
        block = bess[d * per_shard:(d + 1) * per_shard].reshape(span, radii)
        back.append(jnp.dot(left[d], block, preferred_element_type=jnp.float32))
    for i in range(images):
        mine = jnp.concatenate([b[i * half:(i + 1) * half] for b in back], axis=0)
        mine = jnp.transpose(mine).astype(jnp.bfloat16)
        out_ref[i] = jnp.dot(mine, table_ref[...], preferred_element_type=jnp.float32).astype(jnp.bfloat16)


def packed_body(particles, whitening, ctf, group_id, noise_var, bessel):
    images, radii, angles = particles.shape
    freqs, q = bessel.shape[:2]
    groups = ctf.shape[0]
    shards = lax.axis_size("img")
    per_shard = freqs // shards
    step = q // PACK
    order = np.arange(freqs)[:, None] * np.arange(angles)[None, :] % angles
    phase = 2.0 * math.pi / angles * order
    table = np.stack([np.cos(phase), -np.sin(phase)], axis=0) / math.sqrt(angles)
    table = table.reshape(2, shards, per_shard, angles).transpose(1, 0, 2, 3)
    table = jnp.asarray(table.reshape(2 * freqs, angles), dtype=jnp.bfloat16)
    whole = pl.BlockSpec(memory_space=pl.ANY)
    sent = pl.pallas_call(
        functools.partial(project_kernel, per_shard),
        out_shape=jax.ShapeDtypeStruct((shards, 2 * step, 128), jnp.bfloat16),
        in_specs=[pl.BlockSpec(memory_space=pltpu.SMEM), VM, VM, VM, VM, whole],
        out_specs=VM,
        scratch_shapes=[pltpu.VMEM(bessel.shape, jnp.bfloat16), pltpu.SemaphoreType.DMA],
        compiler_params=PARAMS,
        name="project",
    )(group_id, particles, table, ctf, whitening[None, :], bessel)
    arrived = lax.all_to_all(sent, "img", split_axis=0, concat_axis=0, tiled=True)
    noise = jnp.tile(noise_var, LANES // groups)[None, :]
    filtered = pl.pallas_call(
        functools.partial(packed_filter_kernel, groups, shards * images, per_shard),
        out_shape=jax.ShapeDtypeStruct((shards, step, 128), jnp.bfloat16),
        in_specs=[VM, VM],
        out_specs=VM,
        scratch_shapes=filter_scratch(q, shards * SHARE),
        compiler_params=PARAMS,
        name="wiener_filter",
    )(arrived, noise)
    returned = lax.all_to_all(filtered, "img", split_axis=0, concat_axis=0, tiled=True)
    return pl.pallas_call(
        functools.partial(restore_kernel, per_shard),
        out_shape=jax.ShapeDtypeStruct(particles.shape, jnp.bfloat16),
        in_specs=[VM, VM, whole],
        out_specs=VM,
        scratch_shapes=[pltpu.VMEM(bessel.shape, jnp.bfloat16), pltpu.SemaphoreType.DMA],
        compiler_params=PARAMS,
        name="restore",
    )(returned, table, bessel)


def body(particles, whitening, ctf, group_id, noise_var, bessel):
    share = 2 * particles.shape[0] * bessel.shape[0] // lax.axis_size("img")
    if share == SHARE and bessel.shape[1] == SLOTS and lax.axis_size("img") % PACK == 0:
        return packed_body(particles, whitening, ctf, group_id, noise_var, bessel)
    return plain_body(particles, whitening, ctf, group_id, noise_var, bessel)


def plain_body(particles, whitening, ctf, group_id, noise_var, bessel):
    img_count, radii, angles = particles.shape
    freqs, radial = bessel.shape[:2]
    groups = ctf.shape[0]
    shards = lax.axis_size("img")
    per_shard = freqs // shards
    imgs = shards * img_count
    group_range = jnp.arange(groups, dtype=jnp.int32)
    onehot_local = (group_id[:, None] == group_range[None, :]).astype(jnp.float32)
    weight_rows = jnp.dot(onehot_local, ctf, precision=lax.Precision.HIGHEST) * whitening[None, :]
    filtered = (particles.astype(jnp.float32) * weight_rows[:, :, None]).astype(jnp.bfloat16)
    table = angle_table(angles, freqs)
    spectrum = jnp.dot(
        filtered.reshape(img_count * radii, angles),
        table.reshape(angles, 2 * freqs),
        preferred_element_type=jnp.float32,
    )
    spectrum = spectrum.astype(jnp.bfloat16).reshape(img_count, radii, 2, freqs)
    all_ids = lax.all_gather(group_id, "img", axis=0, tiled=True)
    first = lax.axis_index("img") * per_shard
    own_tables = lax.dynamic_slice_in_dim(bessel, first, per_shard, 0)
    payload = spectrum.transpose(3, 0, 2, 1)
    arrived = lax.all_to_all(payload, "img", split_axis=0, concat_axis=1, tiled=True)
    coef = jnp.einsum(
        "kqr,kipr->qkip", own_tables, arrived, preferred_element_type=jnp.float32
    ).astype(jnp.bfloat16)
    kid = jnp.repeat(jnp.arange(per_shard, dtype=jnp.int32), 2 * imgs)[None, :]
    bid = kid * groups + jnp.tile(jnp.repeat(all_ids, 2), per_shard)[None, :]
    noise = jnp.tile(noise_var, LANES // groups)[None, :]
    denoised = wiener_filter(
        coef.reshape(radial, per_shard * 2 * imgs), bid, kid, noise, groups, imgs
    ).reshape(radial, per_shard, imgs, 2)
    outgoing = jnp.einsum(
        "qkip,kqr->kipr", denoised, own_tables, preferred_element_type=jnp.float32
    ).astype(jnp.bfloat16)
    returned = lax.all_to_all(outgoing, "img", split_axis=1, concat_axis=0, tiled=True)
    back = returned.transpose(1, 3, 2, 0)
    cleaned = jnp.dot(
        back.reshape(img_count * radii, 2 * freqs),
        table.reshape(angles, 2 * freqs).T,
        preferred_element_type=jnp.float32,
    )
    return cleaned.astype(jnp.bfloat16).reshape(img_count, radii, angles)


def solution(mesh):
    in_specs = (
        P(("grp", "img"), None, None),
        P(),
        P("grp", None),
        P(("grp", "img")),
        P("grp"),
        P(),
    )
    out_specs = P(("grp", "img"), None, None)
    return jax.shard_map(body, mesh=mesh, in_specs=in_specs, out_specs=out_specs, check_vma=False)
```

```python
import functools
import math

import jax
import jax.numpy as jnp
import numpy as np
from jax import lax
from jax.experimental import pallas as pl
from jax.experimental.pallas import tpu as pltpu
from jax.sharding import PartitionSpec as P

prior_weight = 8.0
SLOTS = 64
LANES = 2 * SLOTS
TILE = 8


def angle_table(angles, freqs):
    theta = jnp.arange(angles, dtype=jnp.int32)
    order = jnp.arange(freqs, dtype=jnp.int32)
    phase = 2.0 * math.pi / angles * (theta[:, None] * order[None, :] % angles).astype(jnp.float32)
    scale = 1.0 / math.sqrt(angles)
    return jnp.stack([jnp.cos(phase) * scale, -jnp.sin(phase) * scale], axis=1).astype(jnp.bfloat16)


def nt_dot(a, b):
    return lax.dot_general(a, b, (((1,), (1,)), ((), ())), preferred_element_type=jnp.float32)


def swap_halves(x):
    return pltpu.roll(x, SLOTS, x.ndim - 1)


def sweep_all(a_ref, c_ref, v_ref, q):
    hq = q // 2
    half = lax.broadcasted_iota(jnp.int32, (TILE, LANES), 1) // SLOTS
    half_w = lax.broadcasted_iota(jnp.int32, (hq, LANES), 1) // SLOTS
    sub_w = lax.broadcasted_iota(jnp.int32, (hq, LANES), 0)
    for kb in range(q // TILE):
        h, base = divmod(kb * TILE, hq)
        in_half = half == h
        rows = [a_ref[kb * TILE + t] for t in range(TILE)]
        for t in range(TILE):
            row = rows[t]
            turned = swap_halves(row)
            c_ref[t, 0:hq] = jnp.where(half_w == 0, row, turned)
            c_ref[t, hq:q] = jnp.where(half_w == 1, row, turned)
            own = jnp.where(in_half, row[base:base + TILE], turned[base:base + TILE])
            inv = 1.0 / own[t:t + 1]
            here = (half_w == h) & (sub_w == base + t)
            scaled = jnp.where(here, -inv, row * inv)
            later = (half_w == h) & (sub_w > base + t) & (sub_w < base + TILE)
            v_ref[t] = jnp.where(later, 0.0, scaled)
            for u in range(TILE):
                if u != t:
                    rows[u] = jnp.where(here, 0.0, rows[u]) - own[u:u + 1] * scaled
            rows[t] = scaled
        vs = [v_ref[t] for t in range(TILE)]
        keep = ~((half_w == h) & (sub_w >= base) & (sub_w < base + TILE))

        def update(i, carry):
            acc = jnp.where(keep, a_ref[i], 0.0)
            for t in range(TILE):
                acc = acc - c_ref[t, pl.ds(i, 1), :] * vs[t]
            a_ref[i] = acc
            return carry

        lax.fori_loop(0, q, update, 0, unroll=4)
        for t in range(TILE):
            a_ref[kb * TILE + t] = rows[t]


def filter_kernel(groups, imgs, coef_ref, bid_ref, kid_ref, noise_ref, out_ref, *scratch):
    coef = coef_ref[...].astype(jnp.float32)
    done = filter_lanes(groups, imgs, coef, bid_ref[...], kid_ref[...], noise_ref[...], *scratch)
    out_ref[...] = done.astype(jnp.bfloat16)


def filter_lanes(groups, imgs, coef, bid, kid, noise, cf_ref, a_ref, c_ref, v_ref, d_ref):
    q, width = coef.shape
    hq = q // 2
    slot = lax.broadcasted_iota(jnp.int32, (LANES, width), 0)
    member = (slot % SLOTS == bid).astype(jnp.float32)
    same = (slot % SLOTS // groups == kid).astype(jnp.float32)
    low = slot < SLOTS
    weights = member + same * (prior_weight / imgs)
    w_lo = jnp.where(low, weights, 0.0).astype(jnp.bfloat16)
    w_hi = jnp.where(low, 0.0, weights).astype(jnp.bfloat16)
    counts = nt_dot(jnp.full((TILE, width), 0.5, jnp.bfloat16), member.astype(jnp.bfloat16))[0:1]
    scale = 1.0 / (counts + prior_weight)
    cf_ref[...] = coef
    jj = lax.broadcasted_iota(jnp.int32, (hq, LANES), 0)
    col = jj + hq * (lax.broadcasted_iota(jnp.int32, (hq, LANES), 1) // SLOTS)

    def gram(blk, carry):
        start = pl.multiple_of(blk * TILE, TILE)
        mine = cf_ref[pl.ds(start, TILE), :]
        total = None
        for part, w in ((0, w_lo), (1, w_hi)):
            other = cf_ref[part * hq:(part + 1) * hq, :]
            prod = (mine[:, None, :] * other[None, :, :]).reshape(TILE * hq, width)
            top = prod.astype(jnp.bfloat16)
            rest = (prod - top.astype(jnp.float32)).astype(jnp.bfloat16)
            s = nt_dot(top, w) + nt_dot(rest, w)
            total = s if total is None else total + s
        total = total.reshape(TILE, hq, LANES) * scale[None]
        for t in range(TILE):
            a_ref[start + t] = total[t] + jnp.where(col == start + t, noise, 0.0)
        return carry

    lax.fori_loop(0, q // TILE, gram, 0)
    sweep_all(a_ref, c_ref, v_ref, q)
    e_lo = jnp.where(low, member, 0.0).astype(jnp.bfloat16)
    e_hi = jnp.where(low, 0.0, member).astype(jnp.bfloat16)

    def apply(blk, carry):
        start = pl.multiple_of(blk * TILE, TILE)
        wien = []
        for t in range(TILE):
            wien.append(noise * a_ref[start + t] + jnp.where(col == start + t, 1.0, 0.0))
        wien = jnp.concatenate(wien, axis=0).astype(jnp.bfloat16)
        spread_lo = jnp.dot(wien, e_lo, preferred_element_type=jnp.float32).reshape(TILE, hq, width)
        spread_hi = jnp.dot(wien, e_hi, preferred_element_type=jnp.float32).reshape(TILE, hq, width)
        prod = spread_lo * cf_ref[0:hq, :][None] + spread_hi * cf_ref[hq:q, :][None]
        d_ref[pl.ds(start, TILE), :] = jnp.sum(prod, axis=1)
        return carry

    lax.fori_loop(0, q // TILE, apply, 0)
    return d_ref[...]


def filter_scratch(q, width):
    hq = q // 2
    return [
        pltpu.VMEM((q, width), jnp.float32),
        pltpu.VMEM((q, hq, LANES), jnp.float32),
        pltpu.VMEM((TILE, q, LANES), jnp.float32),
        pltpu.VMEM((TILE, hq, LANES), jnp.float32),
        pltpu.VMEM((q, width), jnp.float32),
    ]


VM = pl.BlockSpec(memory_space=pltpu.VMEM)
PARAMS = pltpu.CompilerParams(vmem_limit_bytes=32 * 1024 * 1024)


def wiener_filter(coef, bid, kid, noise, groups, imgs):
    q, width = coef.shape
    return pl.pallas_call(
        functools.partial(filter_kernel, groups, imgs),
        out_shape=jax.ShapeDtypeStruct((q, width), jnp.bfloat16),
        in_specs=[VM] * 4,
        out_specs=VM,
        scratch_shapes=filter_scratch(q, width),
        compiler_params=PARAMS,
        name="wiener_filter",
    )(coef, bid, kid, noise)


PACK = 4
SHARE = 128 // PACK


def lane_block(shape):
    return lax.broadcasted_iota(jnp.int32, shape, 1) // SHARE


def pack(tile):
    step = tile.shape[0] // PACK
    where = lane_block((step, 128))
    blocks = []
    for peer in range(PACK):
        out = None
        for j in range(PACK):
            piece = tile[j * step:(j + 1) * step]
            turn = (j - peer) * SHARE % 128
            piece = pltpu.roll(piece, turn, 1) if turn else piece
            out = piece if out is None else jnp.where(where == j, piece, out)
        blocks.append(out)
    return blocks


def unpack(blocks):
    step = blocks[0].shape[0]
    where = lane_block((step, 128))
    rows = []
    for j in range(PACK):
        out = None
        for peer in range(PACK):
            turn = (peer - j) * SHARE % 128
            piece = pltpu.roll(blocks[peer], turn, 1) if turn else blocks[peer]
            out = piece if out is None else jnp.where(where == peer, piece, out)
        rows.append(out)
    return jnp.concatenate(rows, axis=0)


def greet(shards, me):
    barrier = pltpu.get_barrier_semaphore()
    for d in range(shards):
        @pl.when(d != me)
        def _():
            pl.semaphore_signal(
                barrier, inc=1, device_id={"img": d}, device_id_type=pl.DeviceIdType.MESH
            )
    pl.semaphore_wait(barrier, shards - 1)


def to_peer(src_ref, dst_ref, d, me, send_sem, recv_sem):
    return pltpu.make_async_remote_copy(
        src_ref=src_ref.at[d],
        dst_ref=dst_ref.at[me],
        send_sem=send_sem.at[d],
        recv_sem=recv_sem.at[me],
        device_id={"img": d},
        device_id_type=pl.DeviceIdType.MESH,
    )


def from_peer(src_ref, dst_ref, d, send_sem, recv_sem):
    return pltpu.make_async_remote_copy(
        src_ref=src_ref.at[d],
        dst_ref=dst_ref.at[d],
        send_sem=send_sem.at[d],
        recv_sem=recv_sem.at[d],
        device_id={"img": d},
        device_id_type=pl.DeviceIdType.MESH,
    )


def project_kernel(
    per_shard, gid_ref, part_hbm, table_hbm, ctf_hbm, white_hbm, bessel_hbm, out_ref,
    part_ref, table_ref, ctf_ref, white_ref, bess, sent, sem, send_sem, recv_sem,
):
    images = part_ref.shape[0]
    freqs, q, radii = bess.shape
    shards = freqs // per_shard
    me = lax.axis_index("img")
    loads = [
        pltpu.make_async_copy(src, dst, sem.at[n])
        for n, (src, dst) in enumerate((
            (ctf_hbm, ctf_ref), (white_hbm, white_ref), (table_hbm, table_ref),
            (part_hbm, part_ref), (bessel_hbm, bess),
        ))
    ]
    for load in loads:
        load.start()
    greet(shards, me)
    half = 2 * per_shard
    step = q // PACK
    lane = lax.broadcasted_iota(jnp.int32, (q, 128), 1)
    lane_row = lax.broadcasted_iota(jnp.int32, (step, 128), 1) % SHARE // half
    labels = jnp.zeros((step, 128), jnp.float32)
    for i in range(images):
        labels = jnp.where(lane_row == i, gid_ref[i].astype(jnp.float32), labels)
    labels = labels.astype(jnp.bfloat16)
    for load in loads[:4]:
        load.wait()
    table = table_ref[...]
    spec = []
    for i in range(images):
        weight = ctf_ref[pl.ds(gid_ref[i], 1), :] * white_ref[...]
        weight = jnp.transpose(jnp.broadcast_to(weight, (128, radii)))
        weight = jnp.concatenate([weight] * (part_ref.shape[2] // 128), axis=1)
        filtered = (part_ref[i].astype(jnp.float32) * weight).astype(jnp.bfloat16)
        spec.append(nt_dot(table, filtered).astype(jnp.bfloat16))
    loads[4].wait()
    for t in range(shards // PACK):
        rows = []
        for peer in range(PACK):
            d = t * PACK + peer
            for i in range(images):
                rows.append(spec[i][d * half:(d + 1) * half])
        rows = jnp.concatenate(rows, axis=0)
        acc = jnp.zeros((q, 128), jnp.float32)
        for peer in range(PACK):
            d = t * PACK + peer
            block = bess[d * per_shard:(d + 1) * per_shard].reshape(per_shard * q, radii)
            prod = nt_dot(block, rows)
            for kk in range(per_shard):
                here = (lane // SHARE == peer) & (lane % per_shard == kk)
                acc = jnp.where(here, prod[kk * q:(kk + 1) * q], acc)
        for peer, block in enumerate(pack(acc)):
            d = t * PACK + peer
            sent[d, 0:step] = block.astype(jnp.bfloat16)
            sent[d, step:2 * step] = labels

            @pl.when(d != me)
            def _():
                to_peer(sent, out_ref, d, me, send_sem, recv_sem).start()

    out_ref[me] = sent[me]
    for d in range(shards):
        @pl.when(d != me)
        def _():
            from_peer(sent, out_ref, d, send_sem, recv_sem).wait()


def packed_filter_kernel(groups, imgs, per_shard, in_ref, noise_ref, out_ref, *scratch):
    shards, step = in_ref.shape[0], in_ref.shape[1] // 2
    coef, ids = [], []
    for t in range(shards // PACK):
        blocks = [in_ref[t * PACK + peer].astype(jnp.float32) for peer in range(PACK)]
        coef.append(unpack([block[:step] for block in blocks]))
        row = blocks[0][step:step + 1]
        for peer in range(1, PACK):
            row = jnp.where(lane_block((1, 128)) == peer, blocks[peer][step:step + 1], row)
        ids.append(row)
    coef = jnp.concatenate(coef, axis=1)
    ids = jnp.concatenate(ids, axis=1).astype(jnp.int32)
    kid = lax.broadcasted_iota(jnp.int32, ids.shape, 1) % per_shard
    group = lax.broadcasted_iota(jnp.int32, (1, LANES), 1) % groups
    noise = jnp.zeros((1, LANES), jnp.float32)
    for g in range(groups):
        noise = jnp.where(group == g, noise_ref[g], noise)
    done = filter_lanes(groups, imgs, coef, kid * groups + ids, kid, noise, *scratch)
    for t in range(shards // PACK):
        for peer, block in enumerate(pack(done[:, t * 128:(t + 1) * 128])):
            out_ref[t * PACK + peer] = block.astype(jnp.bfloat16)


def restore_kernel(
    per_shard, in_ref, table_hbm, bessel_hbm, out_hbm,
    table_ref, bess, out_ref, held, sem, out_sem, send_sem, recv_sem,
):
    shards = in_ref.shape[0]
    images = out_ref.shape[0]
    q, radii = bess.shape[1:]
    me = lax.axis_index("img")
    loads = [
        pltpu.make_async_copy(table_hbm, table_ref, sem.at[0]),
        pltpu.make_async_copy(bessel_hbm, bess, sem.at[1]),
    ]
    for load in loads:
        load.start()
    greet(shards, me)
    for d in range(shards):
        @pl.when(d != me)
        def _():
            to_peer(in_ref, held, d, me, send_sem, recv_sem).start()
    held[me] = in_ref[me]
    half = 2 * per_shard
    span = per_shard * q
    keep = (
        lax.broadcasted_iota(jnp.int32, (SHARE, span), 0) % per_shard
        == lax.broadcasted_iota(jnp.int32, (SHARE, span), 1) // q
    )
    for load in loads:
        load.wait()
    for d in range(shards):
        @pl.when(d != me)
        def _():
            from_peer(in_ref, held, d, send_sem, recv_sem).wait()
    back = []
    for t in range(shards // PACK):
        tile = unpack([held[t * PACK + peer].astype(jnp.float32) for peer in range(PACK)])
        flat = jnp.transpose(tile)
        for peer in range(PACK):
            d = t * PACK + peer
            mine = flat[peer * SHARE:(peer + 1) * SHARE]
            wide = jnp.concatenate([mine] * per_shard, axis=1)
            left = jnp.where(keep, wide, 0.0).astype(jnp.bfloat16)
            block = bess[d * per_shard:(d + 1) * per_shard].reshape(span, radii)
            back.append(jnp.dot(left, block, preferred_element_type=jnp.float32))
    stores = []
    for i in range(images):
        mine = jnp.concatenate([b[i * half:(i + 1) * half] for b in back], axis=0)
        mine = jnp.transpose(mine).astype(jnp.bfloat16)
        out_ref[i] = jnp.dot(mine, table_ref[...], preferred_element_type=jnp.float32).astype(jnp.bfloat16)
        stores.append(pltpu.make_async_copy(out_ref.at[i], out_hbm.at[i], out_sem.at[i]))
        stores[i].start()
    for store in stores:
        store.wait()


def remote_params(n):
    return pltpu.CompilerParams(
        vmem_limit_bytes=32 * 1024 * 1024, collective_id=n, has_side_effects=True
    )


def packed_body(particles, whitening, ctf, group_id, noise_var, bessel):
    images, radii, angles = particles.shape
    freqs, q = bessel.shape[:2]
    groups = ctf.shape[0]
    shards = lax.axis_size("img")
    per_shard = freqs // shards
    step = q // PACK
    order = np.arange(freqs)[:, None] * np.arange(angles)[None, :] % angles
    phase = 2.0 * math.pi / angles * order
    table = np.stack([np.cos(phase), -np.sin(phase)], axis=0) / math.sqrt(angles)
    table = table.reshape(2, shards, per_shard, angles).transpose(1, 0, 2, 3)
    table = jnp.asarray(table.reshape(2 * freqs, angles), dtype=jnp.bfloat16)
    hbm = pl.BlockSpec(memory_space=pltpu.HBM)
    smem = pl.BlockSpec(memory_space=pltpu.SMEM)
    arrived = pl.pallas_call(
        functools.partial(project_kernel, per_shard),
        out_shape=jax.ShapeDtypeStruct((shards, 2 * step, 128), jnp.bfloat16),
        in_specs=[smem, hbm, hbm, hbm, hbm, hbm],
        out_specs=VM,
        scratch_shapes=[
            pltpu.VMEM(particles.shape, jnp.bfloat16),
            pltpu.VMEM(table.shape, jnp.bfloat16),
            pltpu.VMEM(ctf.shape, jnp.float32),
            pltpu.VMEM((1, radii), jnp.float32),
            pltpu.VMEM(bessel.shape, jnp.bfloat16),
            pltpu.VMEM((shards, 2 * step, 128), jnp.bfloat16),
            pltpu.SemaphoreType.DMA((5,)),
            pltpu.SemaphoreType.DMA((shards,)),
            pltpu.SemaphoreType.DMA((shards,)),
        ],
        compiler_params=remote_params(0),
        name="project",
    )(group_id, particles, table, ctf, whitening[None, :], bessel)
    filtered = pl.pallas_call(
        functools.partial(packed_filter_kernel, groups, shards * images, per_shard),
        out_shape=jax.ShapeDtypeStruct((shards, step, 128), jnp.bfloat16),
        in_specs=[VM, smem],
        out_specs=VM,
        scratch_shapes=filter_scratch(q, shards * SHARE),
        compiler_params=PARAMS,
        name="wiener_filter",
    )(arrived, noise_var)
    return pl.pallas_call(
        functools.partial(restore_kernel, per_shard),
        out_shape=jax.ShapeDtypeStruct(particles.shape, jnp.bfloat16),
        in_specs=[VM, hbm, hbm],
        out_specs=hbm,
        scratch_shapes=[
            pltpu.VMEM(table.shape, jnp.bfloat16),
            pltpu.VMEM(bessel.shape, jnp.bfloat16),
            pltpu.VMEM(particles.shape, jnp.bfloat16),
            pltpu.VMEM((shards, step, 128), jnp.bfloat16),
            pltpu.SemaphoreType.DMA((2,)),
            pltpu.SemaphoreType.DMA((images,)),
            pltpu.SemaphoreType.DMA((shards,)),
            pltpu.SemaphoreType.DMA((shards,)),
        ],
        compiler_params=remote_params(1),
        name="restore",
    )(filtered, table, bessel)


def body(particles, whitening, ctf, group_id, noise_var, bessel):
    share = 2 * particles.shape[0] * bessel.shape[0] // lax.axis_size("img")
    if share == SHARE and bessel.shape[1] == SLOTS and lax.axis_size("img") % PACK == 0:
        return packed_body(particles, whitening, ctf, group_id, noise_var, bessel)
    return plain_body(particles, whitening, ctf, group_id, noise_var, bessel)


def plain_body(particles, whitening, ctf, group_id, noise_var, bessel):
    img_count, radii, angles = particles.shape
    freqs, radial = bessel.shape[:2]
    groups = ctf.shape[0]
    shards = lax.axis_size("img")
    per_shard = freqs // shards
    imgs = shards * img_count
    group_range = jnp.arange(groups, dtype=jnp.int32)
    onehot_local = (group_id[:, None] == group_range[None, :]).astype(jnp.float32)
    weight_rows = jnp.dot(onehot_local, ctf, precision=lax.Precision.HIGHEST) * whitening[None, :]
    filtered = (particles.astype(jnp.float32) * weight_rows[:, :, None]).astype(jnp.bfloat16)
    table = angle_table(angles, freqs)
    spectrum = jnp.dot(
        filtered.reshape(img_count * radii, angles),
        table.reshape(angles, 2 * freqs),
        preferred_element_type=jnp.float32,
    )
    spectrum = spectrum.astype(jnp.bfloat16).reshape(img_count, radii, 2, freqs)
    all_ids = lax.all_gather(group_id, "img", axis=0, tiled=True)
    first = lax.axis_index("img") * per_shard
    own_tables = lax.dynamic_slice_in_dim(bessel, first, per_shard, 0)
    payload = spectrum.transpose(3, 0, 2, 1)
    arrived = lax.all_to_all(payload, "img", split_axis=0, concat_axis=1, tiled=True)
    coef = jnp.einsum(
        "kqr,kipr->qkip", own_tables, arrived, preferred_element_type=jnp.float32
    ).astype(jnp.bfloat16)
    kid = jnp.repeat(jnp.arange(per_shard, dtype=jnp.int32), 2 * imgs)[None, :]
    bid = kid * groups + jnp.tile(jnp.repeat(all_ids, 2), per_shard)[None, :]
    noise = jnp.tile(noise_var, LANES // groups)[None, :]
    denoised = wiener_filter(
        coef.reshape(radial, per_shard * 2 * imgs), bid, kid, noise, groups, imgs
    ).reshape(radial, per_shard, imgs, 2)
    outgoing = jnp.einsum(
        "qkip,kqr->kipr", denoised, own_tables, preferred_element_type=jnp.float32
    ).astype(jnp.bfloat16)
    returned = lax.all_to_all(outgoing, "img", split_axis=1, concat_axis=0, tiled=True)
    back = returned.transpose(1, 3, 2, 0)
    cleaned = jnp.dot(
        back.reshape(img_count * radii, 2 * freqs),
        table.reshape(angles, 2 * freqs).T,
        preferred_element_type=jnp.float32,
    )
    return cleaned.astype(jnp.bfloat16).reshape(img_count, radii, angles)


def solution(mesh):
    in_specs = (
        P(("grp", "img"), None, None),
        P(),
        P("grp", None),
        P(("grp", "img")),
        P("grp"),
        P(),
    )
    out_specs = P(("grp", "img"), None, None)
    return jax.shard_map(body, mesh=mesh, in_specs=in_specs, out_specs=out_specs, check_vma=False)
```

```python
import functools
import math

import jax
import jax.numpy as jnp
import numpy as np
from jax import lax
from jax.experimental import pallas as pl
from jax.experimental.pallas import tpu as pltpu
from jax.sharding import PartitionSpec as P

prior_weight = 8.0
SLOTS = 64
LANES = 2 * SLOTS
TILE = 8
VMEM_LIMIT = 60 * 1024 * 1024


def angle_table(angles, freqs):
    theta = jnp.arange(angles, dtype=jnp.int32)
    order = jnp.arange(freqs, dtype=jnp.int32)
    phase = 2.0 * math.pi / angles * (theta[:, None] * order[None, :] % angles).astype(jnp.float32)
    scale = 1.0 / math.sqrt(angles)
    return jnp.stack([jnp.cos(phase) * scale, -jnp.sin(phase) * scale], axis=1).astype(jnp.bfloat16)


def nt_dot(a, b):
    return lax.dot_general(a, b, (((1,), (1,)), ((), ())), preferred_element_type=jnp.float32)


def swap_halves(x):
    return pltpu.roll(x, SLOTS, x.ndim - 1)


def sweep_all(a_ref, c_ref, v_ref, q):
    hq = q // 2
    half = lax.broadcasted_iota(jnp.int32, (TILE, LANES), 1) // SLOTS
    half_w = lax.broadcasted_iota(jnp.int32, (hq, LANES), 1) // SLOTS
    sub_w = lax.broadcasted_iota(jnp.int32, (hq, LANES), 0)
    for kb in range(q // TILE):
        h, base = divmod(kb * TILE, hq)
        in_half = half == h
        rows = [a_ref[kb * TILE + t] for t in range(TILE)]
        for t in range(TILE):
            row = rows[t]
            turned = swap_halves(row)
            c_ref[t, 0:hq] = jnp.where(half_w == 0, row, turned)
            c_ref[t, hq:q] = jnp.where(half_w == 1, row, turned)
            own = jnp.where(in_half, row[base:base + TILE], turned[base:base + TILE])
            inv = 1.0 / own[t:t + 1]
            here = (half_w == h) & (sub_w == base + t)
            scaled = jnp.where(here, -inv, row * inv)
            later = (half_w == h) & (sub_w > base + t) & (sub_w < base + TILE)
            v_ref[t] = jnp.where(later, 0.0, scaled)
            for u in range(TILE):
                if u != t:
                    rows[u] = jnp.where(here, 0.0, rows[u]) - own[u:u + 1] * scaled
            rows[t] = scaled
        vs = [v_ref[t] for t in range(TILE)]
        keep = ~((half_w == h) & (sub_w >= base) & (sub_w < base + TILE))

        def update(i, carry):
            acc = jnp.where(keep, a_ref[i], 0.0)
            for t in range(TILE):
                acc = acc - c_ref[t, pl.ds(i, 1), :] * vs[t]
            a_ref[i] = acc
            return carry

        lax.fori_loop(0, q, update, 0, unroll=4)
        for t in range(TILE):
            a_ref[kb * TILE + t] = rows[t]


def filter_kernel(groups, imgs, coef_ref, bid_ref, kid_ref, noise_ref, out_ref, *scratch):
    coef = coef_ref[...].astype(jnp.float32)
    done = filter_lanes(groups, imgs, coef, bid_ref[...], kid_ref[...], noise_ref[...], *scratch)
    out_ref[...] = done.astype(jnp.bfloat16)


def filter_lanes(groups, imgs, coef, bid, kid, noise, cf_ref, a_ref, c_ref, v_ref, d_ref):
    q, width = coef.shape
    hq = q // 2
    slot = lax.broadcasted_iota(jnp.int32, (LANES, width), 0)
    member = (slot % SLOTS == bid).astype(jnp.float32)
    same = (slot % SLOTS // groups == kid).astype(jnp.float32)
    low = slot < SLOTS
    weights = member + same * (prior_weight / imgs)
    w_lo = jnp.where(low, weights, 0.0).astype(jnp.bfloat16)
    w_hi = jnp.where(low, 0.0, weights).astype(jnp.bfloat16)
    counts = nt_dot(jnp.full((TILE, width), 0.5, jnp.bfloat16), member.astype(jnp.bfloat16))[0:1]
    scale = 1.0 / (counts + prior_weight)
    cf_ref[...] = coef
    jj = lax.broadcasted_iota(jnp.int32, (hq, LANES), 0)
    col = jj + hq * (lax.broadcasted_iota(jnp.int32, (hq, LANES), 1) // SLOTS)

    def gram(blk, carry):
        start = pl.multiple_of(blk * TILE, TILE)
        mine = cf_ref[pl.ds(start, TILE), :]
        total = None
        for part, w in ((0, w_lo), (1, w_hi)):
            other = cf_ref[part * hq:(part + 1) * hq, :]
            prod = (mine[:, None, :] * other[None, :, :]).reshape(TILE * hq, width)
            top = prod.astype(jnp.bfloat16)
            rest = (prod - top.astype(jnp.float32)).astype(jnp.bfloat16)
            s = nt_dot(top, w) + nt_dot(rest, w)
            total = s if total is None else total + s
        total = total.reshape(TILE, hq, LANES) * scale[None]
        for t in range(TILE):
            a_ref[start + t] = total[t] + jnp.where(col == start + t, noise, 0.0)
        return carry

    lax.fori_loop(0, q // TILE, gram, 0)
    sweep_all(a_ref, c_ref, v_ref, q)
    e_lo = jnp.where(low, member, 0.0).astype(jnp.bfloat16)
    e_hi = jnp.where(low, 0.0, member).astype(jnp.bfloat16)

    def apply(blk, carry):
        start = pl.multiple_of(blk * TILE, TILE)
        wien = []
        for t in range(TILE):
            wien.append(noise * a_ref[start + t] + jnp.where(col == start + t, 1.0, 0.0))
        wien = jnp.concatenate(wien, axis=0).astype(jnp.bfloat16)
        spread_lo = jnp.dot(wien, e_lo, preferred_element_type=jnp.float32).reshape(TILE, hq, width)
        spread_hi = jnp.dot(wien, e_hi, preferred_element_type=jnp.float32).reshape(TILE, hq, width)
        prod = spread_lo * cf_ref[0:hq, :][None] + spread_hi * cf_ref[hq:q, :][None]
        d_ref[pl.ds(start, TILE), :] = jnp.sum(prod, axis=1)
        return carry

    lax.fori_loop(0, q // TILE, apply, 0)
    return d_ref[...]


def filter_scratch(q, width):
    hq = q // 2
    return [
        pltpu.VMEM((q, width), jnp.float32),
        pltpu.VMEM((q, hq, LANES), jnp.float32),
        pltpu.VMEM((TILE, q, LANES), jnp.float32),
        pltpu.VMEM((TILE, hq, LANES), jnp.float32),
        pltpu.VMEM((q, width), jnp.float32),
    ]


VM = pl.BlockSpec(memory_space=pltpu.VMEM)
PARAMS = pltpu.CompilerParams(vmem_limit_bytes=32 * 1024 * 1024)


def wiener_filter(coef, bid, kid, noise, groups, imgs):
    q, width = coef.shape
    return pl.pallas_call(
        functools.partial(filter_kernel, groups, imgs),
        out_shape=jax.ShapeDtypeStruct((q, width), jnp.bfloat16),
        in_specs=[VM] * 4,
        out_specs=VM,
        scratch_shapes=filter_scratch(q, width),
        compiler_params=PARAMS,
        name="wiener_filter",
    )(coef, bid, kid, noise)


PACK = 4
SHARE = 128 // PACK


def lane_block(shape):
    return lax.broadcasted_iota(jnp.int32, shape, 1) // SHARE


def pack(tile):
    step = tile.shape[0] // PACK
    where = lane_block((step, 128))
    blocks = []
    for peer in range(PACK):
        out = None
        for j in range(PACK):
            piece = tile[j * step:(j + 1) * step]
            turn = (j - peer) * SHARE % 128
            piece = pltpu.roll(piece, turn, 1) if turn else piece
            out = piece if out is None else jnp.where(where == j, piece, out)
        blocks.append(out)
    return blocks


def unpack(blocks):
    step = blocks[0].shape[0]
    where = lane_block((step, 128))
    rows = []
    for j in range(PACK):
        out = None
        for peer in range(PACK):
            turn = (peer - j) * SHARE % 128
            piece = pltpu.roll(blocks[peer], turn, 1) if turn else blocks[peer]
            out = piece if out is None else jnp.where(where == peer, piece, out)
        rows.append(out)
    return jnp.concatenate(rows, axis=0)


def greet(shards, me):
    barrier = pltpu.get_barrier_semaphore()
    for d in range(shards):
        @pl.when(d != me)
        def _():
            pl.semaphore_signal(
                barrier, inc=1, device_id={"img": d}, device_id_type=pl.DeviceIdType.MESH
            )
    pl.semaphore_wait(barrier, shards - 1)


def to_peer(src_ref, dst_ref, d, me, send_sem, recv_sem):
    return pltpu.make_async_remote_copy(
        src_ref=src_ref.at[d],
        dst_ref=dst_ref.at[me],
        send_sem=send_sem.at[d],
        recv_sem=recv_sem.at[me],
        device_id={"img": d},
        device_id_type=pl.DeviceIdType.MESH,
    )


def from_peer(src_ref, dst_ref, d, send_sem, recv_sem):
    return pltpu.make_async_remote_copy(
        src_ref=src_ref.at[d],
        dst_ref=dst_ref.at[d],
        send_sem=send_sem.at[d],
        recv_sem=recv_sem.at[d],
        device_id={"img": d},
        device_id_type=pl.DeviceIdType.MESH,
    )


def fused_kernel(
    per_shard, groups, gid_ref, noise_ref, part_hbm, table_hbm, ctf_hbm, white_hbm, bessel_hbm, out_hbm,
    part_ref, table_ref, ctf_ref, white_ref, bess, sent, came, answer, held, out_ref,
    sem, out_sem, send_sem, recv_sem, send_sem2, recv_sem2, *scratch,
):
    images = part_ref.shape[0]
    freqs, q, radii = bess.shape
    shards = freqs // per_shard
    me = lax.axis_index("img")
    loads = [
        pltpu.make_async_copy(src, dst, sem.at[n])
        for n, (src, dst) in enumerate((
            (ctf_hbm, ctf_ref), (white_hbm, white_ref), (table_hbm, table_ref),
            (part_hbm, part_ref), (bessel_hbm, bess),
        ))
    ]
    for load in loads:
        load.start()
    greet(shards, me)
    half = 2 * per_shard
    step = q // PACK
    lane = lax.broadcasted_iota(jnp.int32, (q, 128), 1)
    lane_row = lax.broadcasted_iota(jnp.int32, (step, 128), 1) % SHARE // half
    labels = jnp.zeros((step, 128), jnp.float32)
    for i in range(images):
        labels = jnp.where(lane_row == i, gid_ref[i].astype(jnp.float32), labels)
    labels = labels.astype(jnp.bfloat16)
    for load in loads[:4]:
        load.wait()
    table = table_ref[...]
    spec = []
    for i in range(images):
        weight = ctf_ref[pl.ds(gid_ref[i], 1), :] * white_ref[...]
        weight = jnp.transpose(jnp.broadcast_to(weight, (128, radii)))
        weight = jnp.concatenate([weight] * (part_ref.shape[2] // 128), axis=1)
        filtered = (part_ref[i].astype(jnp.float32) * weight).astype(jnp.bfloat16)
        spec.append(nt_dot(table, filtered).astype(jnp.bfloat16))
    loads[4].wait()
    for t in range(shards // PACK):
        rows = []
        for peer in range(PACK):
            d = t * PACK + peer
            for i in range(images):
                rows.append(spec[i][d * half:(d + 1) * half])
        rows = jnp.concatenate(rows, axis=0)
        acc = jnp.zeros((q, 128), jnp.float32)
        for peer in range(PACK):
            d = t * PACK + peer
            block = bess[d * per_shard:(d + 1) * per_shard].reshape(per_shard * q, radii)
            prod = nt_dot(block, rows)
            for kk in range(per_shard):
                here = (lane // SHARE == peer) & (lane % per_shard == kk)
                acc = jnp.where(here, prod[kk * q:(kk + 1) * q], acc)
        for peer, block in enumerate(pack(acc)):
            d = t * PACK + peer
            sent[d, 0:step] = block.astype(jnp.bfloat16)
            sent[d, step:2 * step] = labels

            @pl.when(d != me)
            def _():
                to_peer(sent, came, d, me, send_sem, recv_sem).start()

    came[me] = sent[me]
    for d in range(shards):
        @pl.when(d != me)
        def _():
            from_peer(sent, came, d, send_sem, recv_sem).wait()

    coef, ids = [], []
    for t in range(shards // PACK):
        blocks = [came[t * PACK + peer].astype(jnp.float32) for peer in range(PACK)]
        coef.append(unpack([block[:step] for block in blocks]))
        row = blocks[0][step:step + 1]
        for peer in range(1, PACK):
            row = jnp.where(lane_block((1, 128)) == peer, blocks[peer][step:step + 1], row)
        ids.append(row)
    coef = jnp.concatenate(coef, axis=1)
    ids = jnp.concatenate(ids, axis=1).astype(jnp.int32)
    kid = lax.broadcasted_iota(jnp.int32, ids.shape, 1) % per_shard
    group = lax.broadcasted_iota(jnp.int32, (1, LANES), 1) % groups
    noise = jnp.zeros((1, LANES), jnp.float32)
    for g in range(groups):
        noise = jnp.where(group == g, noise_ref[g], noise)
    imgs = shards * images
    done = filter_lanes(groups, imgs, coef, kid * groups + ids, kid, noise, *scratch)
    for t in range(shards // PACK):
        for peer, block in enumerate(pack(done[:, t * 128:(t + 1) * 128])):
            d = t * PACK + peer
            answer[d] = block.astype(jnp.bfloat16)

            @pl.when(d != me)
            def _():
                to_peer(answer, held, d, me, send_sem2, recv_sem2).start()
    held[me] = answer[me]
    span = per_shard * q
    keep = (
        lax.broadcasted_iota(jnp.int32, (SHARE, span), 0) % per_shard
        == lax.broadcasted_iota(jnp.int32, (SHARE, span), 1) // q
    )
    back = []
    for t in range(shards // PACK):
        for peer in range(PACK):
            d = t * PACK + peer

            @pl.when(d != me)
            def _():
                from_peer(answer, held, d, send_sem2, recv_sem2).wait()

        tile = unpack([held[t * PACK + peer].astype(jnp.float32) for peer in range(PACK)])
        flat = jnp.transpose(tile)
        for peer in range(PACK):
            d = t * PACK + peer
            mine = flat[peer * SHARE:(peer + 1) * SHARE]
            wide = jnp.concatenate([mine] * per_shard, axis=1)
            left = jnp.where(keep, wide, 0.0).astype(jnp.bfloat16)
            block = bess[d * per_shard:(d + 1) * per_shard].reshape(span, radii)
            back.append(jnp.dot(left, block, preferred_element_type=jnp.float32))
    stores = []
    for i in range(images):
        mine = jnp.concatenate([b[i * half:(i + 1) * half] for b in back], axis=0)
        mine = jnp.transpose(mine).astype(jnp.bfloat16)
        out_ref[i] = jnp.dot(mine, table_ref[...], preferred_element_type=jnp.float32).astype(jnp.bfloat16)
        stores.append(pltpu.make_async_copy(out_ref.at[i], out_hbm.at[i], out_sem.at[i]))
        stores[i].start()
    for store in stores:
        store.wait()


def packed_body(particles, whitening, ctf, group_id, noise_var, bessel):
    images, radii, angles = particles.shape
    freqs, q = bessel.shape[:2]
    groups = ctf.shape[0]
    shards = lax.axis_size("img")
    per_shard = freqs // shards
    step = q // PACK
    order = np.arange(freqs)[:, None] * np.arange(angles)[None, :] % angles
    phase = 2.0 * math.pi / angles * order
    table = np.stack([np.cos(phase), -np.sin(phase)], axis=0) / math.sqrt(angles)
    table = table.reshape(2, shards, per_shard, angles).transpose(1, 0, 2, 3)
    table = jnp.asarray(table.reshape(2 * freqs, angles), dtype=jnp.bfloat16)
    hbm = pl.BlockSpec(memory_space=pltpu.HBM)
    smem = pl.BlockSpec(memory_space=pltpu.SMEM)
    return pl.pallas_call(
        functools.partial(fused_kernel, per_shard, groups),
        out_shape=jax.ShapeDtypeStruct(particles.shape, jnp.bfloat16),
        in_specs=[smem, smem, hbm, hbm, hbm, hbm, hbm],
        out_specs=hbm,
        scratch_shapes=[
            pltpu.VMEM(particles.shape, jnp.bfloat16),
            pltpu.VMEM(table.shape, jnp.bfloat16),
            pltpu.VMEM(ctf.shape, jnp.float32),
            pltpu.VMEM((1, radii), jnp.float32),
            pltpu.VMEM(bessel.shape, jnp.bfloat16),
            pltpu.VMEM((shards, 2 * step, 128), jnp.bfloat16),
            pltpu.VMEM((shards, 2 * step, 128), jnp.bfloat16),
            pltpu.VMEM((shards, step, 128), jnp.bfloat16),
            pltpu.VMEM((shards, step, 128), jnp.bfloat16),
            pltpu.VMEM(particles.shape, jnp.bfloat16),
            pltpu.SemaphoreType.DMA((5,)),
            pltpu.SemaphoreType.DMA((images,)),
            pltpu.SemaphoreType.DMA((shards,)),
            pltpu.SemaphoreType.DMA((shards,)),
            pltpu.SemaphoreType.DMA((shards,)),
            pltpu.SemaphoreType.DMA((shards,)),
        ] + filter_scratch(q, shards * SHARE),
        compiler_params=pltpu.CompilerParams(
            vmem_limit_bytes=VMEM_LIMIT, collective_id=0, has_side_effects=True
        ),
        name="fused",
    )(group_id, noise_var, particles, table, ctf, whitening[None, :], bessel)


def body(particles, whitening, ctf, group_id, noise_var, bessel):
    share = 2 * particles.shape[0] * bessel.shape[0] // lax.axis_size("img")
    if share == SHARE and bessel.shape[1] == SLOTS and lax.axis_size("img") % PACK == 0:
        return packed_body(particles, whitening, ctf, group_id, noise_var, bessel)
    return plain_body(particles, whitening, ctf, group_id, noise_var, bessel)


def plain_body(particles, whitening, ctf, group_id, noise_var, bessel):
    img_count, radii, angles = particles.shape
    freqs, radial = bessel.shape[:2]
    groups = ctf.shape[0]
    shards = lax.axis_size("img")
    per_shard = freqs // shards
    imgs = shards * img_count
    group_range = jnp.arange(groups, dtype=jnp.int32)
    onehot_local = (group_id[:, None] == group_range[None, :]).astype(jnp.float32)
    weight_rows = jnp.dot(onehot_local, ctf, precision=lax.Precision.HIGHEST) * whitening[None, :]
    filtered = (particles.astype(jnp.float32) * weight_rows[:, :, None]).astype(jnp.bfloat16)
    table = angle_table(angles, freqs)
    spectrum = jnp.dot(
        filtered.reshape(img_count * radii, angles),
        table.reshape(angles, 2 * freqs),
        preferred_element_type=jnp.float32,
    )
    spectrum = spectrum.astype(jnp.bfloat16).reshape(img_count, radii, 2, freqs)
    all_ids = lax.all_gather(group_id, "img", axis=0, tiled=True)
    first = lax.axis_index("img") * per_shard
    own_tables = lax.dynamic_slice_in_dim(bessel, first, per_shard, 0)
    payload = spectrum.transpose(3, 0, 2, 1)
    arrived = lax.all_to_all(payload, "img", split_axis=0, concat_axis=1, tiled=True)
    coef = jnp.einsum(
        "kqr,kipr->qkip", own_tables, arrived, preferred_element_type=jnp.float32
    ).astype(jnp.bfloat16)
    kid = jnp.repeat(jnp.arange(per_shard, dtype=jnp.int32), 2 * imgs)[None, :]
    bid = kid * groups + jnp.tile(jnp.repeat(all_ids, 2), per_shard)[None, :]
    noise = jnp.tile(noise_var, LANES // groups)[None, :]
    denoised = wiener_filter(
        coef.reshape(radial, per_shard * 2 * imgs), bid, kid, noise, groups, imgs
    ).reshape(radial, per_shard, imgs, 2)
    outgoing = jnp.einsum(
        "qkip,kqr->kipr", denoised, own_tables, preferred_element_type=jnp.float32
    ).astype(jnp.bfloat16)
    returned = lax.all_to_all(outgoing, "img", split_axis=1, concat_axis=0, tiled=True)
    back = returned.transpose(1, 3, 2, 0)
    cleaned = jnp.dot(
        back.reshape(img_count * radii, 2 * freqs),
        table.reshape(angles, 2 * freqs).T,
        preferred_element_type=jnp.float32,
    )
    return cleaned.astype(jnp.bfloat16).reshape(img_count, radii, angles)


def solution(mesh):
    in_specs = (
        P(("grp", "img"), None, None),
        P(),
        P("grp", None),
        P(("grp", "img")),
        P("grp"),
        P(),
    )
    out_specs = P(("grp", "img"), None, None)
    return jax.shard_map(body, mesh=mesh, in_specs=in_specs, out_specs=out_specs, check_vma=False)
```

```python
import functools
import math

import jax
import jax.numpy as jnp
import numpy as np
from jax import lax
from jax.experimental import pallas as pl
from jax.experimental.pallas import tpu as pltpu
from jax.sharding import PartitionSpec as P

prior_weight = 8.0
SLOTS = 64
LANES = 2 * SLOTS
TILE = 8
VMEM_LIMIT = 60 * 1024 * 1024


def angle_table(angles, freqs):
    theta = jnp.arange(angles, dtype=jnp.int32)
    order = jnp.arange(freqs, dtype=jnp.int32)
    phase = 2.0 * math.pi / angles * (theta[:, None] * order[None, :] % angles).astype(jnp.float32)
    scale = 1.0 / math.sqrt(angles)
    return jnp.stack([jnp.cos(phase) * scale, -jnp.sin(phase) * scale], axis=1).astype(jnp.bfloat16)


def nt_dot(a, b):
    return lax.dot_general(a, b, (((1,), (1,)), ((), ())), preferred_element_type=jnp.float32)


def swap_halves(x):
    return pltpu.roll(x, SLOTS, x.ndim - 1)


def sweep_all(a_ref, c_ref, v_ref, q):
    hq = q // 2
    half = lax.broadcasted_iota(jnp.int32, (TILE, LANES), 1) // SLOTS
    half_w = lax.broadcasted_iota(jnp.int32, (hq, LANES), 1) // SLOTS
    sub_w = lax.broadcasted_iota(jnp.int32, (hq, LANES), 0)
    for kb in range(q // TILE):
        h, base = divmod(kb * TILE, hq)
        in_half = half == h
        rows = [a_ref[kb * TILE + t] for t in range(TILE)]
        for t in range(TILE):
            row = rows[t]
            turned = swap_halves(row)
            c_ref[t, 0:hq] = jnp.where(half_w == 0, row, turned)
            c_ref[t, hq:q] = jnp.where(half_w == 1, row, turned)
            own = jnp.where(in_half, row[base:base + TILE], turned[base:base + TILE])
            inv = 1.0 / own[t:t + 1]
            here = (half_w == h) & (sub_w == base + t)
            scaled = jnp.where(here, -inv, row * inv)
            later = (half_w == h) & (sub_w > base + t) & (sub_w < base + TILE)
            v_ref[t] = jnp.where(later, 0.0, scaled)
            for u in range(TILE):
                if u != t:
                    rows[u] = jnp.where(here, 0.0, rows[u]) - own[u:u + 1] * scaled
            rows[t] = scaled
        vs = [v_ref[t] for t in range(TILE)]
        keep = ~((half_w == h) & (sub_w >= base) & (sub_w < base + TILE))

        def update(i, carry):
            acc = jnp.where(keep, a_ref[i], 0.0)
            for t in range(TILE):
                acc = acc - c_ref[t, pl.ds(i, 1), :] * vs[t]
            a_ref[i] = acc
            return carry

        lax.fori_loop(0, q, update, 0, unroll=8)
        for t in range(TILE):
            a_ref[kb * TILE + t] = rows[t]


def filter_kernel(groups, imgs, coef_ref, bid_ref, kid_ref, noise_ref, out_ref, *scratch):
    coef = coef_ref[...].astype(jnp.float32)
    done = filter_lanes(groups, imgs, coef, bid_ref[...], kid_ref[...], noise_ref[...], *scratch)
    out_ref[...] = done.astype(jnp.bfloat16)


def filter_lanes(groups, imgs, coef, bid, kid, noise, cf_ref, a_ref, c_ref, v_ref, d_ref):
    q, width = coef.shape
    hq = q // 2
    slot = lax.broadcasted_iota(jnp.int32, (LANES, width), 0)
    member = (slot % SLOTS == bid).astype(jnp.float32)
    same = (slot % SLOTS // groups == kid).astype(jnp.float32)
    low = slot < SLOTS
    weights = member + same * (prior_weight / imgs)
    w_lo = jnp.where(low, weights, 0.0).astype(jnp.bfloat16)
    w_hi = jnp.where(low, 0.0, weights).astype(jnp.bfloat16)
    counts = nt_dot(jnp.full((TILE, width), 0.5, jnp.bfloat16), member.astype(jnp.bfloat16))[0:1]
    scale = 1.0 / (counts + prior_weight)
    cf_ref[...] = coef
    jj = lax.broadcasted_iota(jnp.int32, (hq, LANES), 0)
    col = jj + hq * (lax.broadcasted_iota(jnp.int32, (hq, LANES), 1) // SLOTS)

    def gram(blk, carry):
        start = pl.multiple_of(blk * TILE, TILE)
        mine = cf_ref[pl.ds(start, TILE), :]
        total = None
        for part, w in ((0, w_lo), (1, w_hi)):
            other = cf_ref[part * hq:(part + 1) * hq, :]
            prod = (mine[:, None, :] * other[None, :, :]).reshape(TILE * hq, width)
            top = prod.astype(jnp.bfloat16)
            rest = (prod - top.astype(jnp.float32)).astype(jnp.bfloat16)
            s = nt_dot(top, w) + nt_dot(rest, w)
            total = s if total is None else total + s
        total = total.reshape(TILE, hq, LANES) * scale[None]
        for t in range(TILE):
            a_ref[start + t] = total[t] + jnp.where(col == start + t, noise, 0.0)
        return carry

    lax.fori_loop(0, q // TILE, gram, 0, unroll=2)
    sweep_all(a_ref, c_ref, v_ref, q)
    e_lo = jnp.where(low, member, 0.0).astype(jnp.bfloat16)
    e_hi = jnp.where(low, 0.0, member).astype(jnp.bfloat16)

    def apply(blk, carry):
        start = pl.multiple_of(blk * TILE, TILE)
        wien = []
        for t in range(TILE):
            wien.append(noise * a_ref[start + t] + jnp.where(col == start + t, 1.0, 0.0))
        wien = jnp.concatenate(wien, axis=0).astype(jnp.bfloat16)
        spread_lo = jnp.dot(wien, e_lo, preferred_element_type=jnp.float32).reshape(TILE, hq, width)
        spread_hi = jnp.dot(wien, e_hi, preferred_element_type=jnp.float32).reshape(TILE, hq, width)
        prod = spread_lo * cf_ref[0:hq, :][None] + spread_hi * cf_ref[hq:q, :][None]
        d_ref[pl.ds(start, TILE), :] = jnp.sum(prod, axis=1)
        return carry

    lax.fori_loop(0, q // TILE, apply, 0, unroll=2)
    return d_ref[...]


def filter_scratch(q, width):
    hq = q // 2
    return [
        pltpu.VMEM((q, width), jnp.float32),
        pltpu.VMEM((q, hq, LANES), jnp.float32),
        pltpu.VMEM((TILE, q, LANES), jnp.float32),
        pltpu.VMEM((TILE, hq, LANES), jnp.float32),
        pltpu.VMEM((q, width), jnp.float32),
    ]


VM = pl.BlockSpec(memory_space=pltpu.VMEM)
PARAMS = pltpu.CompilerParams(vmem_limit_bytes=32 * 1024 * 1024)


def wiener_filter(coef, bid, kid, noise, groups, imgs):
    q, width = coef.shape
    return pl.pallas_call(
        functools.partial(filter_kernel, groups, imgs),
        out_shape=jax.ShapeDtypeStruct((q, width), jnp.bfloat16),
        in_specs=[VM] * 4,
        out_specs=VM,
        scratch_shapes=filter_scratch(q, width),
        compiler_params=PARAMS,
        name="wiener_filter",
    )(coef, bid, kid, noise)


PACK = 4
SHARE = 128 // PACK


def lane_block(shape):
    return lax.broadcasted_iota(jnp.int32, shape, 1) // SHARE


def pack(tile):
    step = tile.shape[0] // PACK
    where = lane_block((step, 128))
    blocks = []
    for peer in range(PACK):
        out = None
        for j in range(PACK):
            piece = tile[j * step:(j + 1) * step]
            turn = (j - peer) * SHARE % 128
            piece = pltpu.roll(piece, turn, 1) if turn else piece
            out = piece if out is None else jnp.where(where == j, piece, out)
        blocks.append(out)
    return blocks


def unpack(blocks):
    step = blocks[0].shape[0]
    where = lane_block((step, 128))
    rows = []
    for j in range(PACK):
        out = None
        for peer in range(PACK):
            turn = (peer - j) * SHARE % 128
            piece = pltpu.roll(blocks[peer], turn, 1) if turn else blocks[peer]
            out = piece if out is None else jnp.where(where == peer, piece, out)
        rows.append(out)
    return jnp.concatenate(rows, axis=0)


def greet(shards, me):
    barrier = pltpu.get_barrier_semaphore()
    for d in range(shards):
        @pl.when(d != me)
        def _():
            pl.semaphore_signal(
                barrier, inc=1, device_id={"img": d}, device_id_type=pl.DeviceIdType.MESH
            )
    pl.semaphore_wait(barrier, shards - 1)


def to_peer(src_ref, dst_ref, d, me, send_sem, recv_sem):
    return pltpu.make_async_remote_copy(
        src_ref=src_ref.at[d],
        dst_ref=dst_ref.at[me],
        send_sem=send_sem.at[d],
        recv_sem=recv_sem.at[me],
        device_id={"img": d},
        device_id_type=pl.DeviceIdType.MESH,
    )


def from_peer(src_ref, dst_ref, d, send_sem, recv_sem):
    return pltpu.make_async_remote_copy(
        src_ref=src_ref.at[d],
        dst_ref=dst_ref.at[d],
        send_sem=send_sem.at[d],
        recv_sem=recv_sem.at[d],
        device_id={"img": d},
        device_id_type=pl.DeviceIdType.MESH,
    )


def fused_kernel(
    per_shard, groups, gid_ref, noise_ref, part_hbm, table_hbm, ctf_hbm, white_hbm, bessel_hbm, out_hbm,
    part_ref, table_ref, ctf_ref, white_ref, bess, sent, came, answer, held, out_ref,
    sem, out_sem, send_sem, recv_sem, send_sem2, recv_sem2, *scratch,
):
    images = part_ref.shape[0]
    freqs, q, radii = bess.shape
    shards = freqs // per_shard
    me = lax.axis_index("img")
    loads = [
        pltpu.make_async_copy(src, dst, sem.at[n])
        for n, (src, dst) in enumerate((
            (ctf_hbm, ctf_ref), (white_hbm, white_ref), (table_hbm, table_ref),
            (part_hbm, part_ref), (bessel_hbm, bess),
        ))
    ]
    for load in loads:
        load.start()
    greet(shards, me)
    half = 2 * per_shard
    step = q // PACK
    lane = lax.broadcasted_iota(jnp.int32, (q, 128), 1)
    lane_row = lax.broadcasted_iota(jnp.int32, (step, 128), 1) % SHARE // half
    labels = jnp.zeros((step, 128), jnp.float32)
    for i in range(images):
        labels = jnp.where(lane_row == i, gid_ref[i].astype(jnp.float32), labels)
    labels = labels.astype(jnp.bfloat16)
    for load in loads[:4]:
        load.wait()
    table = table_ref[...]
    spec = []
    for i in range(images):
        weight = ctf_ref[pl.ds(gid_ref[i], 1), :] * white_ref[...]
        weight = jnp.transpose(jnp.broadcast_to(weight, (128, radii)))
        weight = jnp.concatenate([weight] * (part_ref.shape[2] // 128), axis=1)
        filtered = (part_ref[i].astype(jnp.float32) * weight).astype(jnp.bfloat16)
        spec.append(nt_dot(table, filtered).astype(jnp.bfloat16))
    loads[4].wait()
    for t in range(shards // PACK):
        rows = []
        for peer in range(PACK):
            d = t * PACK + peer
            for i in range(images):
                rows.append(spec[i][d * half:(d + 1) * half])
        rows = jnp.concatenate(rows, axis=0)
        acc = jnp.zeros((q, 128), jnp.float32)
        for peer in range(PACK):
            d = t * PACK + peer
            block = bess[d * per_shard:(d + 1) * per_shard].reshape(per_shard * q, radii)
            prod = nt_dot(block, rows)
            for kk in range(per_shard):
                here = (lane // SHARE == peer) & (lane % per_shard == kk)
                acc = jnp.where(here, prod[kk * q:(kk + 1) * q], acc)
        for peer, block in enumerate(pack(acc)):
            d = t * PACK + peer
            sent[d, 0:step] = block.astype(jnp.bfloat16)
            sent[d, step:2 * step] = labels

            @pl.when(d != me)
            def _():
                to_peer(sent, came, d, me, send_sem, recv_sem).start()

    came[me] = sent[me]
    for d in range(shards):
        @pl.when(d != me)
        def _():
            from_peer(sent, came, d, send_sem, recv_sem).wait()

    coef, ids = [], []
    for t in range(shards // PACK):
        blocks = [came[t * PACK + peer].astype(jnp.float32) for peer in range(PACK)]
        coef.append(unpack([block[:step] for block in blocks]))
        row = blocks[0][step:step + 1]
        for peer in range(1, PACK):
            row = jnp.where(lane_block((1, 128)) == peer, blocks[peer][step:step + 1], row)
        ids.append(row)
    coef = jnp.concatenate(coef, axis=1)
    ids = jnp.concatenate(ids, axis=1).astype(jnp.int32)
    kid = lax.broadcasted_iota(jnp.int32, ids.shape, 1) % per_shard
    group = lax.broadcasted_iota(jnp.int32, (1, LANES), 1) % groups
    noise = jnp.zeros((1, LANES), jnp.float32)
    for g in range(groups):
        noise = jnp.where(group == g, noise_ref[g], noise)
    imgs = shards * images
    done = filter_lanes(groups, imgs, coef, kid * groups + ids, kid, noise, *scratch)
    for t in range(shards // PACK):
        for peer, block in enumerate(pack(done[:, t * 128:(t + 1) * 128])):
            d = t * PACK + peer
            answer[d] = block.astype(jnp.bfloat16)

            @pl.when(d != me)
            def _():
                to_peer(answer, held, d, me, send_sem2, recv_sem2).start()
    held[me] = answer[me]
    span = per_shard * q
    keep = (
        lax.broadcasted_iota(jnp.int32, (SHARE, span), 0) % per_shard
        == lax.broadcasted_iota(jnp.int32, (SHARE, span), 1) // q
    )
    back = []
    for t in range(shards // PACK):
        for peer in range(PACK):
            d = t * PACK + peer

            @pl.when(d != me)
            def _():
                from_peer(answer, held, d, send_sem2, recv_sem2).wait()

        tile = unpack([held[t * PACK + peer].astype(jnp.float32) for peer in range(PACK)])
        flat = jnp.transpose(tile)
        for peer in range(PACK):
            d = t * PACK + peer
            mine = flat[peer * SHARE:(peer + 1) * SHARE]
            wide = jnp.concatenate([mine] * per_shard, axis=1)
            left = jnp.where(keep, wide, 0.0).astype(jnp.bfloat16)
            block = bess[d * per_shard:(d + 1) * per_shard].reshape(span, radii)
            back.append(jnp.dot(left, block, preferred_element_type=jnp.float32))
    stores = []
    for i in range(images):
        mine = jnp.concatenate([b[i * half:(i + 1) * half] for b in back], axis=0)
        mine = jnp.transpose(mine).astype(jnp.bfloat16)
        out_ref[i] = jnp.dot(mine, table_ref[...], preferred_element_type=jnp.float32).astype(jnp.bfloat16)
        stores.append(pltpu.make_async_copy(out_ref.at[i], out_hbm.at[i], out_sem.at[i]))
        stores[i].start()
    for store in stores:
        store.wait()


def packed_body(particles, whitening, ctf, group_id, noise_var, bessel):
    images, radii, angles = particles.shape
    freqs, q = bessel.shape[:2]
    groups = ctf.shape[0]
    shards = lax.axis_size("img")
    per_shard = freqs // shards
    step = q // PACK
    order = np.arange(freqs)[:, None] * np.arange(angles)[None, :] % angles
    phase = 2.0 * math.pi / angles * order
    table = np.stack([np.cos(phase), -np.sin(phase)], axis=0) / math.sqrt(angles)
    table = table.reshape(2, shards, per_shard, angles).transpose(1, 0, 2, 3)
    table = jnp.asarray(table.reshape(2 * freqs, angles), dtype=jnp.bfloat16)
    hbm = pl.BlockSpec(memory_space=pltpu.HBM)
    smem = pl.BlockSpec(memory_space=pltpu.SMEM)
    return pl.pallas_call(
        functools.partial(fused_kernel, per_shard, groups),
        out_shape=jax.ShapeDtypeStruct(particles.shape, jnp.bfloat16),
        in_specs=[smem, smem, hbm, hbm, hbm, hbm, hbm],
        out_specs=hbm,
        scratch_shapes=[
            pltpu.VMEM(particles.shape, jnp.bfloat16),
            pltpu.VMEM(table.shape, jnp.bfloat16),
            pltpu.VMEM(ctf.shape, jnp.float32),
            pltpu.VMEM((1, radii), jnp.float32),
            pltpu.VMEM(bessel.shape, jnp.bfloat16),
            pltpu.VMEM((shards, 2 * step, 128), jnp.bfloat16),
            pltpu.VMEM((shards, 2 * step, 128), jnp.bfloat16),
            pltpu.VMEM((shards, step, 128), jnp.bfloat16),
            pltpu.VMEM((shards, step, 128), jnp.bfloat16),
            pltpu.VMEM(particles.shape, jnp.bfloat16),
            pltpu.SemaphoreType.DMA((5,)),
            pltpu.SemaphoreType.DMA((images,)),
            pltpu.SemaphoreType.DMA((shards,)),
            pltpu.SemaphoreType.DMA((shards,)),
            pltpu.SemaphoreType.DMA((shards,)),
            pltpu.SemaphoreType.DMA((shards,)),
        ] + filter_scratch(q, shards * SHARE),
        compiler_params=pltpu.CompilerParams(
            vmem_limit_bytes=VMEM_LIMIT, collective_id=0, has_side_effects=True
        ),
        name="fused",
    )(group_id, noise_var, particles, table, ctf, whitening[None, :], bessel)


def body(particles, whitening, ctf, group_id, noise_var, bessel):
    share = 2 * particles.shape[0] * bessel.shape[0] // lax.axis_size("img")
    if share == SHARE and bessel.shape[1] == SLOTS and lax.axis_size("img") % PACK == 0:
        return packed_body(particles, whitening, ctf, group_id, noise_var, bessel)
    return plain_body(particles, whitening, ctf, group_id, noise_var, bessel)


def plain_body(particles, whitening, ctf, group_id, noise_var, bessel):
    img_count, radii, angles = particles.shape
    freqs, radial = bessel.shape[:2]
    groups = ctf.shape[0]
    shards = lax.axis_size("img")
    per_shard = freqs // shards
    imgs = shards * img_count
    group_range = jnp.arange(groups, dtype=jnp.int32)
    onehot_local = (group_id[:, None] == group_range[None, :]).astype(jnp.float32)
    weight_rows = jnp.dot(onehot_local, ctf, precision=lax.Precision.HIGHEST) * whitening[None, :]
    filtered = (particles.astype(jnp.float32) * weight_rows[:, :, None]).astype(jnp.bfloat16)
    table = angle_table(angles, freqs)
    spectrum = jnp.dot(
        filtered.reshape(img_count * radii, angles),
        table.reshape(angles, 2 * freqs),
        preferred_element_type=jnp.float32,
    )
    spectrum = spectrum.astype(jnp.bfloat16).reshape(img_count, radii, 2, freqs)
    all_ids = lax.all_gather(group_id, "img", axis=0, tiled=True)
    first = lax.axis_index("img") * per_shard
    own_tables = lax.dynamic_slice_in_dim(bessel, first, per_shard, 0)
    payload = spectrum.transpose(3, 0, 2, 1)
    arrived = lax.all_to_all(payload, "img", split_axis=0, concat_axis=1, tiled=True)
    coef = jnp.einsum(
        "kqr,kipr->qkip", own_tables, arrived, preferred_element_type=jnp.float32
    ).astype(jnp.bfloat16)
    kid = jnp.repeat(jnp.arange(per_shard, dtype=jnp.int32), 2 * imgs)[None, :]
    bid = kid * groups + jnp.tile(jnp.repeat(all_ids, 2), per_shard)[None, :]
    noise = jnp.tile(noise_var, LANES // groups)[None, :]
    denoised = wiener_filter(
        coef.reshape(radial, per_shard * 2 * imgs), bid, kid, noise, groups, imgs
    ).reshape(radial, per_shard, imgs, 2)
    outgoing = jnp.einsum(
        "qkip,kqr->kipr", denoised, own_tables, preferred_element_type=jnp.float32
    ).astype(jnp.bfloat16)
    returned = lax.all_to_all(outgoing, "img", split_axis=1, concat_axis=0, tiled=True)
    back = returned.transpose(1, 3, 2, 0)
    cleaned = jnp.dot(
        back.reshape(img_count * radii, 2 * freqs),
        table.reshape(angles, 2 * freqs).T,
        preferred_element_type=jnp.float32,
    )
    return cleaned.astype(jnp.bfloat16).reshape(img_count, radii, angles)


def solution(mesh):
    in_specs = (
        P(("grp", "img"), None, None),
        P(),
        P("grp", None),
        P(("grp", "img")),
        P("grp"),
        P(),
    )
    out_specs = P(("grp", "img"), None, None)
    return jax.shard_map(body, mesh=mesh, in_specs=in_specs, out_specs=out_specs, check_vma=False)
```
